32 devices in a mesh: group: 2 (over y), req: 8 (over z, x), tp: 2 (over core).
Axes of the slice: x: 2, y: 2, z: 4, core: 2. Of those that a mesh axis runs over, the one named last changes fastest.
Arguments:
- hidden: bfloat16 [64, 16384], P(('group', 'req')), parts along dimension 0, may hold values from -6 to 6
- adapter_ids: int32 [64], P('group'), parts along dimension 0, may hold values from 0 to 63
- home_slot: int32 [64], replicated, may hold values from 0 to 63, as said below
- lengths: int32 [64], P(('group', 'req')), parts along dimension 0, may hold values from 2 to 512, as said below
- query: bfloat16 [64, 2048], P(('group', 'req'), 'tp'), parts along dimension 0, may hold values from -128 to 128
- kv_base: bfloat16 [64, 256], P(('group', 'req')), parts along dimension 0, may hold values from -6 to 6
- cache: bfloat16 [64, 512, 256], P(('group', 'req')), parts along dimension 0, may hold values from -5 to 5
- adapter_down: bfloat16 [16384, 1024], P('req', 'tp'), may hold values from -0.046875 to 0.046875
- adapter_up: bfloat16 [64, 16, 256], P('req', 'tp'), may hold values from -3 to 3
Outputs:
- new_kv: bfloat16 [64, 256], P(('group', 'req')), parts along dimension 0
- attended: bfloat16 [64, 2048], P(('group', 'req'), 'tp'), parts along dimension 0
The draws below stay inside these ranges and needn't reach their ends.
There are 2 independent parts, one for each index of `group`. The reference program is written for one: setup_inputs(seed, part) draws one part's arguments, and reference() takes and returns one part's arrays. A program takes and returns all parts, laid end to end along the dimension named above; an argument that names none is the same for every part. Nothing has to cross between parts.
Inputs may be any that keep to these rules, and one draw needn't show every extreme that they name: `home_slot`: distinct bank slots; slots 0 and 63 always hold an adapter. `lengths`: some request reaches 512.
All inputs are finite; a program needn't handle non-finite values.
Results may differ from the reference program's by a relative error of at most 0.02.
Values may be sent and summed in bfloat16 or wider, within the bound.
No kernel may reach another device: no remote copies, remote signals or barrier semaphores. Data moves between devices by JAX's collectives and lax.ppermute only.
A program may use at most 64 MiB of HBM per device.

```python
import math
import jax
import jax.numpy as jnp
import numpy as np

D = 16384
HD = 128
QH = 16
R = 16
ADAPTERS = 64
L = 512
REQS = 32
BANK = 64


def cache_base(key):
    return jax.random.truncated_normal(key, -4.0, 4.0, (REQS, L, 2 * HD), jnp.float32)


def draw_cache(key, part):
    base = cache_base(key)
    return base.astype(jnp.bfloat16)


def draw_query(key, part):
    key = jax.random.fold_in(key, 23)
    query = jax.random.truncated_normal(key, -4.0, 4.0, (REQS, QH, HD), jnp.float32)
    return query.reshape(REQS, QH * HD).astype(jnp.bfloat16)


def draw_lengths(key, part):
    key = jax.random.fold_in(key, 37)
    first, second = jax.random.split(key)
    values = jax.random.randint(first, (REQS,), 2, L + 1)
    where = jax.random.randint(second, (), 0, REQS)
    return values.at[where].set(L).astype(jnp.int32)


def draw_home_slot(key, part):
    key = jax.random.fold_in(key, 53)
    first, second = jax.random.split(key)
    middle = jax.random.permutation(first, BANK - 2)[:ADAPTERS - 2] + 1
    values = jnp.concatenate([jnp.array([0, BANK - 1], jnp.int32), middle.astype(jnp.int32)])
    return jax.random.permutation(second, values).astype(jnp.int32)


def with_ends(drawn, own_key, least, high):
    longest = drawn.shape.index(max(drawn.shape))
    spots = []
    for shift in (0, 1):
        where = [jax.random.randint(jax.random.fold_in(own_key, axis), (), 0, length) for axis, length in enumerate(drawn.shape)]
        where[longest] = (where[longest] + shift) % drawn.shape[longest]
        spots.append(tuple(where))
    return drawn.at[spots[0]].set(least).at[spots[1]].set(high)


def level_of(stream_key, dims, cuts, least, largest):
    def one(position, shards_of):
        heights = jax.random.uniform(jax.random.fold_in(jax.random.fold_in(stream_key, 6), position), (shards_of,), jnp.float32, least / len(cuts), largest / len(cuts))
        return jnp.repeat(jnp.exp(heights), dims[position] // shards_of).reshape((-1,) + (1,) * (len(dims) - position - 1))

    gain = one(*cuts[0])
    for cut in cuts[1:]:
        gain = gain * one(*cut)
    return gain


def rank_bounds(amount, lean):
    weights = [(1 << 20) // math.isqrt(rank ** lean) + 1 for rank in range(1, amount + 1)]
    deviation = 1 + sum(weights) // (1 << 30)
    return np.cumsum(np.array([max(1, weight // deviation) for weight in weights]))


def ranked_ids(own_key, extent, amount, lean):
    listing = rank_bounds(amount, lean)
    lot = jax.random.randint(jax.random.fold_in(own_key, 1), extent, 0, int(listing[amount - 1]))
    rank = jnp.searchsorted(jnp.asarray(listing, jnp.int32), lot, side="right")
    return jax.random.permutation(jax.random.fold_in(own_key, 2), amount)[rank].astype(jnp.int32)


def normal_values(own_key, extent, spread, most, shards=(), kind=jnp.bfloat16):
    values = spread * jax.random.normal(own_key, extent, jnp.float32)
    if shards:
        values = values * level_of(own_key, extent, shards, -0.22, 0.18)
    return jnp.clip(values, -most, most).astype(kind)


def setup_inputs(seed: int = 0, part: int = 0) -> dict:
    seeds = jax.random.split(jax.random.key(seed), 10)
    part_keys = jax.random.split(jax.random.fold_in(seeds[9], part), 10)
    return {
        "hidden": normal_values(part_keys[0], (REQS, D), 1.0, 6.0, ((0, 8),)),
        "adapter_ids": with_ends(ranked_ids(part_keys[1], (REQS,), ADAPTERS, 2), jax.random.fold_in(part_keys[1], 3), 0, ADAPTERS - 1).astype(jnp.int32),
        "home_slot": draw_home_slot(jax.random.fold_in(seeds[9], 71), part),
        "lengths": draw_lengths(jax.random.fold_in(jax.random.fold_in(seeds[9], part), 71), part),
        "query": draw_query(jax.random.fold_in(jax.random.fold_in(seeds[9], part), 71), part),
        "kv_base": normal_values(part_keys[5], (REQS, 2 * HD), 1.0, 6.0, ((0, 8),)),
        "cache": draw_cache(jax.random.fold_in(jax.random.fold_in(seeds[9], part), 71), part),
        "adapter_down": normal_values(seeds[7], (D, R * ADAPTERS), D ** -0.5, 0.046875, ((0, 8), (1, 2))),
        "adapter_up": normal_values(seeds[8], (BANK, R, 2 * HD), (R // 4) ** -0.5, 3.0, ((0, 8), (1, 2))),
    }


def attend(query, cache, new_kv, lengths):
    count = query.shape[0]
    heads = query.shape[1] // HD
    scale = HD ** -0.5
    q_rows = query.reshape(count, heads, HD)
    keys = cache[:, :, :HD]
    values = cache[:, :, HD:]
    k_new = new_kv[:, :HD]
    v_new = new_kv[:, HD:]
    scores = jnp.einsum("bhd,bld->bhl", q_rows.astype(jnp.float32), keys.astype(jnp.float32)) * scale
    valid = jnp.arange(cache.shape[1], dtype=jnp.int32)[None, None, :] < lengths[:, None, None]
    scores = jnp.where(valid, scores, -jnp.inf)
    own = jnp.einsum("bhd,bd->bh", q_rows.astype(jnp.float32), k_new.astype(jnp.float32)) * scale
    top = jnp.maximum(jnp.max(scores, axis=-1), own)
    weights = jnp.exp(scores - top[:, :, None])
    own_weight = jnp.exp(own - top)
    total = jnp.sum(weights, axis=-1) + own_weight
    probs = (weights / total[:, :, None]).astype(jnp.bfloat16)
    own_p = (own_weight / total).astype(jnp.bfloat16)
    result = jnp.einsum("bhl,bld->bhd", probs.astype(jnp.float32), values.astype(jnp.float32))
    result = result + own_p.astype(jnp.float32)[:, :, None] * v_new.astype(jnp.float32)[:, None, :]
    return result.reshape(count, heads * HD).astype(jnp.bfloat16)


def reference(hidden, adapter_ids, home_slot, lengths, query, kv_base, cache, adapter_down, adapter_up):
    projected = jnp.dot(hidden, adapter_down, preferred_element_type=jnp.float32)
    projected = projected.reshape(REQS, R, ADAPTERS)
    picker = (adapter_ids[:, None] == jnp.arange(ADAPTERS, dtype=jnp.int32)[None, :]).astype(jnp.float32)
    low = jnp.einsum("bra,ba->br", projected, picker)
    low_b = low.astype(jnp.bfloat16)
    rows = adapter_up[home_slot[adapter_ids]]
    delta = jnp.einsum("br,brk->bk", low_b.astype(jnp.float32), rows.astype(jnp.float32))
    new_kv = (kv_base.astype(jnp.float32) + delta).astype(jnp.bfloat16)
    attended = attend(query, cache, new_kv, lengths)
    return new_kv, attended
```

```python
import jax
import jax.numpy as jnp
from jax import lax
from jax.sharding import PartitionSpec as P

HD = 128
ADAPTERS = 64


def cached_part(query, cache, lengths):
    count = query.shape[0]
    heads = query.shape[1] // HD
    scale = HD ** (-0.5)
    q_rows = query.reshape(count, heads, HD)
    keys = cache[:, :, :HD]
    values = cache[:, :, HD:]
    scores = jnp.einsum("bhd,bld->bhl", q_rows, keys, preferred_element_type=jnp.float32) * scale
    valid = jnp.arange(cache.shape[1], dtype=jnp.int32)[None, None, :] < lengths[:, None, None]
    scores = jnp.where(valid, scores, -jnp.inf)
    top = jnp.max(scores, axis=-1)
    weights = jnp.exp(scores - top[:, :, None])
    total = jnp.sum(weights, axis=-1)
    result = jnp.einsum(
        "bhl,bld->bhd", weights.astype(jnp.bfloat16), values, preferred_element_type=jnp.float32
    )
    return q_rows, top, total, result


def merge_own(q_rows, top, total, result, new_kv):
    count, heads, _ = q_rows.shape
    scale = HD ** (-0.5)
    k_new = new_kv[:, :HD].astype(jnp.float32)
    v_new = new_kv[:, HD:].astype(jnp.float32)
    own = jnp.sum(q_rows.astype(jnp.float32) * k_new[:, None, :], axis=-1) * scale
    high = jnp.maximum(top, own)
    keep = jnp.exp(top - high)
    own_weight = jnp.exp(own - high)
    norm = 1.0 / (total * keep + own_weight)
    out = result * (keep * norm)[:, :, None] + (own_weight * norm)[:, :, None] * v_new[:, None, :]
    return out.reshape(count, heads * HD).astype(jnp.bfloat16)


def shards(
    hidden, adapter_ids, home_slot, lengths, query, kv_base, cache, adapter_down, adapter_up
):
    per_dev = hidden.shape[0]
    slots, ranks, width = adapter_up.shape
    parts = lax.axis_size("req")
    me = lax.axis_index("req")
    everyone = per_dev * parts
    block = lax.all_to_all(hidden, "req", split_axis=1, concat_axis=0, tiled=True)
    picker = adapter_ids[:, None] == jnp.arange(ADAPTERS, dtype=jnp.int32)[None, :]
    wanted = jnp.sum(jnp.where(picker, home_slot[None, :], 0), axis=1) - me * slots
    mine = (wanted[:, None] == jnp.arange(slots, dtype=jnp.int32)[None, :]).astype(jnp.bfloat16)
    rows = jnp.dot(
        mine, adapter_up.reshape(slots, ranks * width), preferred_element_type=jnp.float32
    ).astype(jnp.bfloat16)
    rows = rows.reshape(parts, per_dev * ranks * width)
    q_rows, top, total, result = cached_part(query, cache, lengths)
    projected = jnp.dot(block, adapter_down, preferred_element_type=jnp.float32)
    projected = projected.reshape(everyone, ranks, ADAPTERS)
    low_part = jnp.sum(jnp.where(picker[:, None, :], projected, 0.0), axis=2)
    high = low_part.astype(jnp.bfloat16)
    rest = (low_part - high.astype(jnp.float32)).astype(jnp.bfloat16)
    packed = jnp.concatenate(
        [
            rows,
            high.reshape(parts, per_dev * ranks),
            rest.reshape(parts, per_dev * ranks),
        ],
        axis=1,
    )
    got = lax.all_to_all(packed, "req", split_axis=0, concat_axis=0, tiled=True)
    got = jnp.sum(got.astype(jnp.float32), axis=0)
    size = per_dev * ranks
    up_rows = got[: size * width].reshape(per_dev, ranks, width)
    low = (got[size * width : size * width + size] + got[size * width + size :]).astype(jnp.bfloat16)
    low = low.reshape(per_dev, ranks).astype(jnp.float32)
    delta = jnp.sum(low[:, :, None] * up_rows, axis=1)
    delta = delta + lax.ppermute(delta, "tp", [(0, 1), (1, 0)])
    new_kv = (kv_base.astype(jnp.float32) + delta).astype(jnp.bfloat16)
    attended = merge_own(q_rows, top, total, result, new_kv)
    return (new_kv, attended)


def solution(mesh):
    placed = (
        P(("group", "req"), None),
        P("group"),
        P(),
        P(("group", "req")),
        P(("group", "req"), "tp"),
        P(("group", "req"), None),
        P(("group", "req"), None, None),
        P("req", "tp"),
        P("req", "tp", None),
    )
    return jax.shard_map(
        shards,
        mesh=mesh,
        in_specs=placed,
        out_specs=(P(("group", "req"), None), P(("group", "req"), "tp")),
        check_vma=False,
    )
```

```python
import functools

import jax
import jax.numpy as jnp
from jax import lax
from jax.experimental import pallas as pl
from jax.experimental.pallas import tpu as pltpu
from jax.sharding import PartitionSpec as P

HD = 128
ADAPTERS = 64
F32 = jnp.float32
BF16 = jnp.bfloat16
VMEM = pl.BlockSpec(memory_space=pltpu.VMEM)
SMEM = pl.BlockSpec(memory_space=pltpu.SMEM)
HBM = pl.BlockSpec(memory_space=pltpu.HBM)
PARAMS = pltpu.CompilerParams(vmem_limit_bytes=8 * 1024 * 1024)


def iota(shape, dim):
    return lax.broadcasted_iota(jnp.int32, shape, dim)


def one_hot_ids(ids):
    shape = (ADAPTERS, ids.shape[1])
    return (iota(shape, 0) == jnp.broadcast_to(ids, shape)).astype(BF16)


def across(a, b):
    return lax.dot_general(a, b, (((0,), (0,)), ((), ())), preferred_element_type=F32)


def rotate_kernel(order, hidden_ref, out_ref, held_ref, sems):
    block = out_ref.shape[2]
    copies = [
        pltpu.make_async_copy(
            hidden_ref.at[:, pl.ds(q * block, block)], held_ref.at[p], sems.at[p]
        )
        for p, q in enumerate(order)
    ]
    for copy in copies:
        copy.start()
    for copy in copies:
        copy.wait()
    copy = pltpu.make_async_copy(held_ref, out_ref, sems.at[0])
    copy.start()
    copy.wait()


def local_kernel(
    order, base_ref, lengths_ref, ids_hbm, home_hbm, query_hbm, up_hbm, cache_hbm, down_hbm,
    q_ref, acc_ref, top_ref, total_ref, rows_ref, pick_ref, down_ref,
    ids_ref, home_ref, query_ref, up_ref, cache_ref, flat_ref, wide_ref, sems
):
    pairs = (
        (ids_hbm, ids_ref),
        (home_hbm, home_ref),
        (query_hbm, query_ref),
        (up_hbm, up_ref),
        (cache_hbm, cache_ref),
        (down_hbm, down_ref),
    )
    copies = [pltpu.make_async_copy(a, b, sems.at[i]) for i, (a, b) in enumerate(pairs)]
    for copy in copies:
        copy.start()
    for copy in copies[:4]:
        copy.wait()
    slots, ranks, width = up_ref.shape
    depth = flat_ref.shape[0]
    count = cache_ref.shape[0]
    heads = query_ref.shape[1] // HD
    scale = HD ** (-0.5)
    chosen_ids = one_hot_ids(ids_ref[...])
    if depth > slots:
        flat_ref[...] = jnp.zeros_like(flat_ref)
    wide_ref[...] = up_ref[...].astype(F32)
    for r in range(ranks):
        flat_ref[:slots, r * width : (r + 1) * width] = wide_ref[:, r, :]
    shape = (depth, ADAPTERS)
    here = jnp.broadcast_to(home_ref[...], shape) - base_ref[0] == iota(shape, 0)
    held = here & (iota(shape, 0) < slots)
    match = jnp.dot(held.astype(BF16), chosen_ids, preferred_element_type=F32)
    rows = across(match.astype(BF16), flat_ref[...].astype(BF16)).astype(BF16)
    columns = pick_ref.shape[1]
    spread = (iota((ADAPTERS, columns), 1) % ADAPTERS == iota((ADAPTERS, columns), 0)).astype(BF16)
    pick = across(chosen_ids, spread)
    shift = order[0] * count
    if shift:
        pick = jnp.concatenate([pick[shift:], pick[:shift]], axis=0)
    pick_ref[...] = pick
    for p, q in enumerate(order):
        rows_ref[p] = rows[q * count : (q + 1) * count]
    query = query_ref[...].astype(F32)
    for h in range(heads):
        q_ref[pl.ds(h, count, stride=heads), :] = query[:, h * HD : (h + 1) * HD]
    copies[4].wait()
    for b in range(count):
        part = pl.ds(b * heads, heads)
        scores = lax.dot_general(
            q_ref[part, :].astype(BF16),
            cache_ref[b, :, :HD],
            (((1,), (1,)), ((), ())),
            preferred_element_type=F32,
        )
        valid = iota(scores.shape, 1) < lengths_ref[b]
        scores = jnp.where(valid, scores * scale, -jnp.inf)
        top = jnp.max(scores, axis=1, keepdims=True)
        weights = jnp.exp(scores - top)
        total = jnp.sum(weights, axis=1, keepdims=True)
        acc_ref[part, :] = jnp.dot(
            weights.astype(BF16), cache_ref[b, :, HD:], preferred_element_type=F32
        )
        top_ref[part, :] = jnp.broadcast_to(top, (heads, HD))
        total_ref[part, :] = jnp.broadcast_to(total, (heads, HD))
    copies[5].wait()


def low_kernel(ranks, block_ref, down_ref, pick_ref, rows_ref, out_ref):
    parts, per_dev, _ = out_ref.shape
    span = rows_ref.shape[2]
    projected = jnp.dot(block_ref[...], down_ref[...], preferred_element_type=F32)
    chosen = projected * pick_ref[...]
    high = chosen.astype(BF16)
    rest = (chosen - high.astype(F32)).astype(BF16)
    columns = chosen.shape[1]
    ends = (iota((columns, 128), 0) // ADAPTERS, iota((columns, 128), 1))
    fold = (ends[0] == ends[1]).astype(BF16)
    fold_rest = (ends[0] + ranks == ends[1]).astype(BF16)
    low = jnp.dot(high, fold, preferred_element_type=F32)
    low = low + jnp.dot(rest, fold_rest, preferred_element_type=F32)
    low = low.astype(BF16)
    for p in range(parts):
        out_ref[p, :, :span] = rows_ref[p]
        out_ref[p, :, span:] = low[p * per_dev : (p + 1) * per_dev]


def delta_kernel(ranks, got_ref, out_ref):
    parts, count, _ = got_ref.shape
    width = out_ref.shape[1]
    got = got_ref[0].astype(F32)
    for p in range(1, parts):
        got = got + got_ref[p].astype(F32)
    low = got[:, ranks * width :]
    delta = jnp.zeros((count, width), F32)
    for r in range(ranks):
        share = (low[:, r : r + 1] + low[:, r + ranks : r + ranks + 1]).astype(BF16).astype(F32)
        delta = delta + share * got[:, r * width : (r + 1) * width]
    out_ref[...] = delta


def merge_kernel(
    mine_ref, other_ref, base_ref, q_ref, acc_ref, top_ref, total_ref, kv_ref, out_ref, wide_ref
):
    count = base_ref.shape[0]
    heads = q_ref.shape[0] // count
    scale = HD ** (-0.5)
    delta = mine_ref[...] + other_ref[...]
    new_kv = (base_ref[...].astype(F32) + delta).astype(BF16)
    kv_ref[...] = new_kv
    fresh = new_kv.astype(F32)
    for b in range(count):
        rows = pl.ds(b * heads, heads)
        key = fresh[b : b + 1, :HD]
        value = fresh[b : b + 1, HD:]
        own = jnp.sum(q_ref[rows, :] * key, axis=1, keepdims=True) * scale
        own = jnp.broadcast_to(own, (heads, HD))
        top = top_ref[rows, :]
        high = jnp.maximum(top, own)
        keep = jnp.exp(top - high)
        weight = jnp.exp(own - high)
        norm = 1.0 / (total_ref[rows, :] * keep + weight)
        wide_ref[rows, :] = (acc_ref[rows, :] * keep + weight * value) * norm
    for h in range(heads):
        out_ref[:, h * HD : (h + 1) * HD] = wide_ref[pl.ds(h, count, stride=heads), :].astype(BF16)


def shards(
    hidden, adapter_ids, home_slot, lengths, query, kv_base, cache, adapter_down, adapter_up
):
    per_dev = hidden.shape[0]
    slots, ranks, width = adapter_up.shape
    parts = lax.axis_size("req")
    everyone = per_dev * parts
    block = hidden.shape[1] // parts
    heads = query.shape[1] // HD
    center = (parts // 2 + 1) % parts
    order = [(center + p) % parts for p in range(parts)]
    depth = -(-slots // 8) * 8
    base = (lax.axis_index("req") * slots).astype(jnp.int32).reshape(1)
    span = ranks * width
    pin = lambda x: pltpu.with_memory_space_constraint(x, pltpu.HBM)
    blocks = pl.pallas_call(
        functools.partial(rotate_kernel, order),
        out_shape=jax.ShapeDtypeStruct((parts, per_dev, block), BF16),
        in_specs=[HBM],
        out_specs=HBM,
        scratch_shapes=[
            pltpu.VMEM((parts, per_dev, block), BF16),
            pltpu.SemaphoreType.DMA((parts,)),
        ],
        compiler_params=PARAMS,
    )(pin(hidden))
    blocks = lax.all_to_all(
        blocks, "req", split_axis=0, concat_axis=0, tiled=True, axis_index_groups=[order]
    )
    small = jax.ShapeDtypeStruct((per_dev * heads, HD), F32)
    q_rows, acc, top, total, rows, pick, down = pl.pallas_call(
        functools.partial(local_kernel, order),
        out_shape=(small, small, small, small)
        + (
            jax.ShapeDtypeStruct((parts, per_dev, span), BF16),
            jax.ShapeDtypeStruct((everyone, ranks * ADAPTERS), F32),
            jax.ShapeDtypeStruct(adapter_down.shape, BF16),
        ),
        in_specs=[SMEM, SMEM] + [HBM] * 6,
        out_specs=(VMEM,) * 7,
        scratch_shapes=[
            pltpu.VMEM((1, everyone), jnp.int32),
            pltpu.VMEM((1, ADAPTERS), jnp.int32),
            pltpu.VMEM(query.shape, BF16),
            pltpu.VMEM(adapter_up.shape, BF16),
            pltpu.VMEM(cache.shape, BF16),
            pltpu.VMEM((depth, span), F32),
            pltpu.VMEM((slots, ranks, width), F32),
            pltpu.SemaphoreType.DMA((6,)),
        ],
        compiler_params=PARAMS,
    )(
        base,
        lengths,
        pin(adapter_ids.reshape(1, everyone)),
        pin(home_slot.reshape(1, ADAPTERS)),
        pin(query),
        pin(adapter_up),
        pin(cache),
        pin(adapter_down),
    )
    packed = pl.pallas_call(
        functools.partial(low_kernel, ranks),
        out_shape=jax.ShapeDtypeStruct((parts, per_dev, span + 128), BF16),
        in_specs=[VMEM] * 4,
        out_specs=VMEM,
        compiler_params=PARAMS,
    )(blocks.reshape(everyone, block), down, pick, rows)
    got = lax.all_to_all(
        packed, "req", split_axis=0, concat_axis=0, tiled=True, axis_index_groups=[order]
    )
    delta = pl.pallas_call(
        functools.partial(delta_kernel, ranks),
        out_shape=jax.ShapeDtypeStruct((per_dev, width), F32),
        in_specs=[VMEM],
        out_specs=VMEM,
        compiler_params=PARAMS,
    )(got)
    other = lax.ppermute(delta, "tp", [(0, 1), (1, 0)])
    new_kv, attended = pl.pallas_call(
        merge_kernel,
        out_shape=(
            jax.ShapeDtypeStruct(kv_base.shape, BF16),
            jax.ShapeDtypeStruct(query.shape, BF16),
        ),
        in_specs=[VMEM] * 7,
        out_specs=(VMEM, VMEM),
        scratch_shapes=[pltpu.VMEM((per_dev * heads, HD), F32)],
        compiler_params=PARAMS,
    )(delta, other, kv_base, q_rows, acc, top, total)
    return (new_kv, attended)


def solution(mesh):
    placed = (
        P(("group", "req"), None),
        P("group"),
        P(),
        P(("group", "req")),
        P(("group", "req"), "tp"),
        P(("group", "req"), None),
        P(("group", "req"), None, None),
        P("req", "tp"),
        P("req", "tp", None),
    )
    return jax.shard_map(
        shards,
        mesh=mesh,
        in_specs=placed,
        out_specs=(P(("group", "req"), None), P(("group", "req"), "tp")),
        check_vma=False,
    )
```

```python
import functools

import jax
import jax.numpy as jnp
from jax import lax
from jax.experimental import pallas as pl
from jax.experimental.pallas import tpu as pltpu
from jax.sharding import PartitionSpec as P

HD = 128
ADAPTERS = 64
F32 = jnp.float32
BF16 = jnp.bfloat16
VMEM = pl.BlockSpec(memory_space=pltpu.VMEM)
SMEM = pl.BlockSpec(memory_space=pltpu.SMEM)
HBM = pl.BlockSpec(memory_space=pltpu.HBM)
PARAMS = pltpu.CompilerParams(vmem_limit_bytes=8 * 1024 * 1024)


def iota(shape, dim):
    return lax.broadcasted_iota(jnp.int32, shape, dim)


def one_hot_ids(ids):
    shape = (ADAPTERS, ids.shape[1])
    return (iota(shape, 0) == jnp.broadcast_to(ids, shape)).astype(BF16)


def across(a, b):
    return lax.dot_general(a, b, (((0,), (0,)), ((), ())), preferred_element_type=F32)


def rotate_kernel(order, hidden_ref, out_ref, sems):
    block = out_ref.shape[2]
    copies = [
        pltpu.make_async_copy(
            hidden_ref.at[:, pl.ds(q * block, block)], out_ref.at[p], sems.at[p]
        )
        for p, q in enumerate(order)
    ]
    for copy in copies:
        copy.start()
    for copy in copies:
        copy.wait()


def pack_kernel(
    order, base_ref, ids_hbm, home_hbm, up_hbm, far_hbm, out_ref,
    ids_ref, home_ref, up_ref, far_ref, flat_ref, wide_ref, sems
):
    pairs = ((ids_hbm, ids_ref), (home_hbm, home_ref), (up_hbm, up_ref), (far_hbm, far_ref))
    copies = [pltpu.make_async_copy(a, b, sems.at[i]) for i, (a, b) in enumerate(pairs)]
    for copy in copies:
        copy.start()
    for copy in copies:
        copy.wait()
    slots, ranks, width = up_ref.shape
    depth = flat_ref.shape[0]
    count = out_ref.shape[1]
    if depth > slots:
        flat_ref[...] = jnp.zeros_like(flat_ref)
    for half, ref in enumerate((up_ref, far_ref)):
        wide_ref[...] = ref[...].astype(F32)
        for r in range(ranks):
            at = (half * ranks + r) * width
            flat_ref[:slots, at : at + width] = wide_ref[:, r, :]
    shape = (depth, ADAPTERS)
    here = jnp.broadcast_to(home_ref[...], shape) - base_ref[0] == iota(shape, 0)
    held = here & (iota(shape, 0) < slots)
    match = jnp.dot(held.astype(BF16), one_hot_ids(ids_ref[...]), preferred_element_type=F32)
    rows = across(match.astype(BF16), flat_ref[...].astype(BF16)).astype(BF16)
    for p, q in enumerate(order):
        out_ref[p] = rows[q * count : (q + 1) * count]


def attend_kernel(
    lengths_ref, query_hbm, far_hbm, cache_hbm, mine_ref, far_ref,
    query_ref, cache_ref, q_ref, sems
):
    pairs = ((query_hbm, query_ref.at[0]), (far_hbm, query_ref.at[1]), (cache_hbm, cache_ref))
    copies = [pltpu.make_async_copy(a, b, sems.at[i]) for i, (a, b) in enumerate(pairs)]
    for copy in copies:
        copy.start()
    for copy in copies:
        copy.wait()
    count = cache_ref.shape[0]
    heads = query_ref.shape[2] // HD
    scale = HD ** (-0.5)
    for half in range(2):
        query = query_ref[half].astype(F32)
        for h in range(heads):
            q_ref[pl.ds(half * heads + h, count, stride=2 * heads), :] = query[
                :, h * HD : (h + 1) * HD
            ]
    for b in range(count):
        scores = lax.dot_general(
            q_ref[b * 2 * heads : (b + 1) * 2 * heads, :].astype(BF16),
            cache_ref[b, :, :HD],
            (((1,), (1,)), ((), ())),
            preferred_element_type=F32,
        )
        valid = iota(scores.shape, 1) < lengths_ref[b]
        scores = jnp.where(valid, scores * scale, -jnp.inf)
        top = jnp.max(scores, axis=1, keepdims=True)
        weights = jnp.exp(scores - top)
        total = jnp.sum(weights, axis=1, keepdims=True)
        acc = jnp.dot(weights.astype(BF16), cache_ref[b, :, HD:], preferred_element_type=F32)
        both = jnp.where(iota(acc.shape, 1) < HD // 2, top, total)
        at = b * heads
        for half, ref in enumerate((mine_ref, far_ref)):
            part = slice(half * heads, (half + 1) * heads)
            ref[at : at + heads, :] = acc[part]
            ref[(count + b) * heads : (count + b + 1) * heads, :] = both[part]


def gather_kernel(got_ref, stats_ref, out_ref):
    total = got_ref[0].astype(F32)
    for p in range(1, got_ref.shape[0]):
        total = total + got_ref[p].astype(F32)
    count, span = total.shape
    for j in range(span // HD):
        out_ref[j * count : (j + 1) * count, :] = total[:, j * HD : (j + 1) * HD]
    out_ref[span // HD * count :, :] = stats_ref[...]


def spare_kernel(*refs):
    pass


def low_kernel(order, ids_ref, block_ref, down_ref, far_hbm, out_ref, far_ref, sems):
    parts, per_dev, _ = out_ref.shape
    depth, columns = down_ref.shape
    ranks = columns // ADAPTERS
    pieces = sems.shape[0]
    step = depth // pieces
    copies = [
        pltpu.make_async_copy(
            far_hbm.at[pl.ds(i * step, step)], far_ref.at[pl.ds(i * step, step)], sems.at[i]
        )
        for i in range(pieces)
    ]
    for copy in copies:
        copy.start()
    names = across(one_hot_ids(ids_ref[...]), iota((ADAPTERS, 128), 0).astype(BF16))
    names = names.astype(jnp.int32)
    shift = order[0] * per_dev
    if shift:
        names = jnp.concatenate([names[shift:], names[:shift]], axis=0)
    lane = iota(names.shape, 1)
    spot = names + lane % 2 * ADAPTERS
    rank = lane % (2 * ranks)

    def take(values, half, low):
        for j in range(columns // 128):
            got = jnp.take_along_axis(values[:, j * 128 : (j + 1) * 128], spot, axis=1)
            low = jnp.where(rank // 2 == j + half * ranks // 2, got, low)
        return low

    near = jnp.dot(block_ref[...], down_ref[...], preferred_element_type=F32)
    low = take(near, 1, jnp.zeros(names.shape, F32))
    far = jnp.zeros(near.shape, F32)
    for i in range(pieces):
        copies[i].wait()
        part = slice(i * step, (i + 1) * step)
        far = far + jnp.dot(block_ref[:, part], far_ref[part, :], preferred_element_type=F32)
    low = take(far, 0, low)
    high = low.astype(BF16).astype(F32)
    low = jnp.where(lane < 2 * ranks, high, low - high).astype(BF16)
    for p in range(parts):
        out_ref[p] = low[p * per_dev : (p + 1) * per_dev]


def total_kernel(ranks, got_ref, out_ref):
    total = got_ref[0].astype(F32)
    for p in range(1, got_ref.shape[0]):
        total = total + got_ref[p].astype(F32)
    total = total + pltpu.roll(total, 128 - 2 * ranks, 1)
    out_ref[: total.shape[0], :] = total.astype(BF16).astype(F32)


def merge_kernel(
    ranks, mine_ref, other_ref, stats_ref, base_ref, query_ref,
    kv_ref, out_ref, q_ref, wide_ref
):
    count, width = base_ref.shape
    heads = query_ref.shape[1] // HD
    halves = width // HD
    scale = HD ** (-0.5)
    lower = lax.axis_index("tp") == 0
    tile = halves * count
    span = 2 * ranks * tile
    query = query_ref[...].astype(F32)
    for h in range(heads):
        q_ref[pl.ds(h, count, stride=heads), :] = query[:, h * HD : (h + 1) * HD]
    low = jnp.where(lower, other_ref[:count, :], mine_ref[:count, :])
    low = jnp.concatenate([low] * halves, axis=0)
    base = base_ref[...].astype(F32)
    fresh = jnp.concatenate([base[:, j * HD : (j + 1) * HD] for j in range(halves)], axis=0)
    for r in range(2 * ranks):
        part = slice(r * tile, (r + 1) * tile)
        row = jnp.where(lower, mine_ref[part, :], other_ref[part, :])
        fresh = fresh + low[:, r : r + 1] * row
    fresh = fresh.astype(BF16).astype(F32)
    for j in range(halves):
        kv_ref[:, j * HD : (j + 1) * HD] = fresh[j * count : (j + 1) * count].astype(BF16)
    for b in range(count):
        part = slice(b * heads, (b + 1) * heads)
        far = slice(span + b * heads, span + (b + 1) * heads)
        key = fresh[b : b + 1]
        value = fresh[count + b : count + b + 1]
        own = jnp.sum(q_ref[part, :] * key, axis=1, keepdims=True) * scale
        acc = jnp.where(lower, stats_ref[part, :], other_ref[far, :])
        part = slice((count + b) * heads, (count + b + 1) * heads)
        far = slice(span + (count + b) * heads, span + (count + b + 1) * heads)
        both = jnp.where(lower, stats_ref[part, :], other_ref[far, :])
        top = both[:, :1]
        high = jnp.maximum(top, own)
        keep = jnp.exp(top - high)
        weight = jnp.exp(own - high)
        norm = 1.0 / (both[:, HD - 1 :] * keep + weight)
        part = slice(b * heads, (b + 1) * heads)
        wide_ref[part, :] = acc * (keep * norm) + (weight * norm) * value
    for h in range(heads):
        out_ref[:, h * HD : (h + 1) * HD] = wide_ref[pl.ds(h, count, stride=heads), :].astype(BF16)


def shards(
    hidden, adapter_ids, home_slot, lengths, query, kv_base, cache, adapter_down, adapter_up
):
    per_dev = hidden.shape[0]
    slots, ranks, width = adapter_up.shape
    parts = lax.axis_size("req")
    everyone = per_dev * parts
    block = hidden.shape[1] // parts
    heads = query.shape[1] // HD
    span = 2 * ranks * width
    center = (parts // 2 + 1) % parts
    order = [(center + p) % parts for p in range(parts)]
    depth = -(-slots // 8) * 8
    base = (lax.axis_index("req") * slots).astype(jnp.int32).reshape(1)
    core = lax.axis_index("tp").astype(jnp.int32)
    swap = [(0, 1), (1, 0)]
    stats_shape = jax.ShapeDtypeStruct((2 * per_dev * heads, HD), F32)
    trade_shape = jax.ShapeDtypeStruct((span // HD * per_dev + 2 * per_dev * heads, HD), F32)
    blocks_shape = jax.ShapeDtypeStruct((parts, per_dev, block), BF16)

    def pin(x):
        return pltpu.with_memory_space_constraint(x, pltpu.HBM)

    def exchange(x):
        return lax.all_to_all(
            x, "req", split_axis=0, concat_axis=0, tiled=True, axis_index_groups=[order]
        )

    ids = adapter_ids.reshape(1, everyone)
    far_up = lax.ppermute(adapter_up, "tp", swap)
    far_query = lax.ppermute(query, "tp", swap)
    blocks = pl.pallas_call(
        functools.partial(rotate_kernel, order),
        out_shape=blocks_shape,
        in_specs=[HBM],
        out_specs=VMEM,
        scratch_shapes=[pltpu.SemaphoreType.DMA((parts,))],
        cost_estimate=pl.CostEstimate(flops=0, transcendentals=0, bytes_accessed=1 << 23),
        compiler_params=PARAMS,
    )(pin(hidden))
    far_up, far_query, down, blocks = lax.optimization_barrier(
        (far_up, far_query, adapter_down, blocks)
    )
    far_down = lax.ppermute(down, "tp", swap)

    def lower(blocks, far_up, far_query, lengths, ids, query, cache, home, up, base):
        packed = pl.pallas_call(
            functools.partial(pack_kernel, order),
            out_shape=jax.ShapeDtypeStruct((parts, per_dev, span), BF16),
            in_specs=[SMEM] + [HBM] * 4,
            out_specs=VMEM,
            scratch_shapes=[
                pltpu.VMEM((1, everyone), jnp.int32),
                pltpu.VMEM((1, ADAPTERS), jnp.int32),
                pltpu.VMEM(up.shape, BF16),
                pltpu.VMEM(up.shape, BF16),
                pltpu.VMEM((depth, span), F32),
                pltpu.VMEM((slots, ranks, width), F32),
                pltpu.SemaphoreType.DMA((4,)),
            ],
            compiler_params=PARAMS,
        )(base, pin(ids), pin(home), pin(up), pin(far_up))
        got = exchange(packed)
        mine, far = pl.pallas_call(
            attend_kernel,
            out_shape=(stats_shape, stats_shape),
            in_specs=[SMEM] + [HBM] * 3,
            out_specs=(VMEM, VMEM),
            scratch_shapes=[
                pltpu.VMEM((2,) + query.shape, BF16),
                pltpu.VMEM(cache.shape, BF16),
                pltpu.VMEM((2 * per_dev * heads, HD), F32),
                pltpu.SemaphoreType.DMA((3,)),
            ],
            compiler_params=PARAMS,
        )(lengths, pin(query), pin(far_query), pin(cache))
        trade = pl.pallas_call(
            gather_kernel,
            out_shape=trade_shape,
            in_specs=[VMEM, VMEM],
            out_specs=VMEM,
            compiler_params=PARAMS,
        )(got, far)
        return blocks, mine, trade

    def upper(blocks, far_up, far_query, lengths, ids, query, cache, home, up, base):
        got = exchange(blocks)
        mine, trade = pl.pallas_call(
            spare_kernel,
            out_shape=(stats_shape, trade_shape),
            in_specs=[VMEM],
            out_specs=(VMEM, VMEM),
            compiler_params=PARAMS,
        )(got)
        return got, mine, trade

    got, stats, trade = lax.cond(
        core == 1, upper, lower,
        blocks, far_up, far_query, lengths, ids, query, cache,
        home_slot.reshape(1, ADAPTERS), adapter_up, base,
    )
    pieces = 4 if block % 64 == 0 else 1

    def upper_low(ids, got, down, far_down, trade):
        low = pl.pallas_call(
            functools.partial(low_kernel, order),
            out_shape=jax.ShapeDtypeStruct((parts, per_dev, 128), BF16),
            in_specs=[VMEM] * 3 + [HBM],
            out_specs=VMEM,
            scratch_shapes=[
                pltpu.VMEM(adapter_down.shape, BF16),
                pltpu.SemaphoreType.DMA((pieces,)),
            ],
            compiler_params=PARAMS,
        )(ids, got, down, pin(far_down))
        return pl.pallas_call(
            functools.partial(total_kernel, ranks),
            out_shape=trade_shape,
            in_specs=[VMEM],
            out_specs=VMEM,
            compiler_params=PARAMS,
        )(exchange(low))

    def lower_low(ids, got, down, far_down, trade):
        return trade

    mine = lax.cond(
        core == 1, upper_low, lower_low,
        ids, got.reshape(everyone, block), adapter_down, far_down, trade,
    )
    other = lax.ppermute(mine, "tp", swap)
    new_kv, attended = pl.pallas_call(
        functools.partial(merge_kernel, ranks),
        out_shape=(
            jax.ShapeDtypeStruct(kv_base.shape, BF16),
            jax.ShapeDtypeStruct(query.shape, BF16),
        ),
        in_specs=[VMEM] * 5,
        out_specs=(VMEM, VMEM),
        scratch_shapes=[
            pltpu.VMEM((per_dev * heads, HD), F32),
            pltpu.VMEM((per_dev * heads, HD), F32),
        ],
        compiler_params=PARAMS,
    )(mine, other, stats, kv_base, query)
    return (new_kv, attended)


def solution(mesh):
    placed = (
        P(("group", "req"), None),
        P("group"),
        P(),
        P(("group", "req")),
        P(("group", "req"), "tp"),
        P(("group", "req"), None),
        P(("group", "req"), None, None),
        P("req", "tp"),
        P("req", "tp", None),
    )
    return jax.shard_map(
        shards,
        mesh=mesh,
        in_specs=placed,
        out_specs=(P(("group", "req"), None), P(("group", "req"), "tp")),
        check_vma=False,
    )
```

```python
import functools

import jax
import jax.numpy as jnp
from jax import lax
from jax.experimental import pallas as pl
from jax.experimental.pallas import tpu as pltpu
from jax.sharding import PartitionSpec as P

HD = 128
ADAPTERS = 64
F32 = jnp.float32
BF16 = jnp.bfloat16
VMEM = pl.BlockSpec(memory_space=pltpu.VMEM)
SMEM = pl.BlockSpec(memory_space=pltpu.SMEM)
HBM = pl.BlockSpec(memory_space=pltpu.HBM)
PARAMS = pltpu.CompilerParams(vmem_limit_bytes=8 * 1024 * 1024)


def iota(shape, dim):
    return lax.broadcasted_iota(jnp.int32, shape, dim)


def one_hot_ids(ids):
    shape = (ADAPTERS, ids.shape[1])
    return (iota(shape, 0) == jnp.broadcast_to(ids, shape)).astype(BF16)


def across(a, b):
    return lax.dot_general(a, b, (((0,), (0,)), ((), ())), preferred_element_type=F32)


def rotate_kernel(order, hidden_ref, out_ref, sems):
    block = out_ref.shape[2]

    @pl.when(lax.axis_index("tp") == 1)
    def _():
        copies = [
            pltpu.make_async_copy(
                hidden_ref.at[:, pl.ds(q * block, block)], out_ref.at[p], sems.at[p]
            )
            for p, q in enumerate(order)
        ]
        for copy in copies:
            copy.start()
        for copy in copies:
            copy.wait()


def pack_kernel(
    order, base_ref, ids_hbm, home_hbm, up_hbm, far_ref, out_ref,
    ids_ref, home_ref, up_ref, flat_ref, wide_ref, sems
):
    pairs = ((ids_hbm, ids_ref), (home_hbm, home_ref), (up_hbm, up_ref))
    copies = [pltpu.make_async_copy(a, b, sems.at[i]) for i, (a, b) in enumerate(pairs)]
    for copy in copies:
        copy.start()
    for copy in copies:
        copy.wait()
    slots, ranks, width = up_ref.shape
    depth = flat_ref.shape[0]
    count = out_ref.shape[1]
    if depth > slots:
        flat_ref[...] = jnp.zeros_like(flat_ref)
    for half, ref in enumerate((up_ref, far_ref)):
        wide_ref[...] = ref[...].astype(F32)
        for r in range(ranks):
            at = (half * ranks + r) * width
            flat_ref[:slots, at : at + width] = wide_ref[:, r, :]
    shape = (depth, ADAPTERS)
    here = jnp.broadcast_to(home_ref[...], shape) - base_ref[0] == iota(shape, 0)
    held = here & (iota(shape, 0) < slots)
    match = jnp.dot(held.astype(BF16), one_hot_ids(ids_ref[...]), preferred_element_type=F32)
    rows = across(match.astype(BF16), flat_ref[...].astype(BF16)).astype(BF16)
    for p, q in enumerate(order):
        out_ref[p] = rows[q * count : (q + 1) * count]


def attend_kernel(
    lengths_ref, query_hbm, far_query_ref, cache_hbm, mine_ref, far_ref,
    query_ref, cache_ref, q_ref, sems
):
    pairs = ((query_hbm, query_ref), (cache_hbm, cache_ref))
    copies = [pltpu.make_async_copy(a, b, sems.at[i]) for i, (a, b) in enumerate(pairs)]
    for copy in copies:
        copy.start()
    for copy in copies:
        copy.wait()
    count = cache_ref.shape[0]
    heads = query_ref.shape[1] // HD
    scale = HD ** (-0.5)
    for half, ref in enumerate((query_ref, far_query_ref)):
        query = ref[...].astype(F32)
        for h in range(heads):
            q_ref[pl.ds(half * heads + h, count, stride=2 * heads), :] = query[
                :, h * HD : (h + 1) * HD
            ]
    for b in range(count):
        scores = lax.dot_general(
            q_ref[b * 2 * heads : (b + 1) * 2 * heads, :].astype(BF16),
            cache_ref[b, :, :HD],
            (((1,), (1,)), ((), ())),
            preferred_element_type=F32,
        )
        valid = iota(scores.shape, 1) < lengths_ref[b]
        scores = jnp.where(valid, scores * scale, -jnp.inf)
        top = jnp.max(scores, axis=1, keepdims=True)
        weights = jnp.exp(scores - top)
        total = jnp.sum(weights, axis=1, keepdims=True)
        acc = jnp.dot(weights.astype(BF16), cache_ref[b, :, HD:], preferred_element_type=F32)
        both = jnp.where(iota(acc.shape, 1) < HD // 2, top, total)
        at = b * heads
        for half, ref in enumerate((mine_ref, far_ref)):
            part = slice(half * heads, (half + 1) * heads)
            ref[at : at + heads, :] = acc[part]
            ref[(count + b) * heads : (count + b + 1) * heads, :] = both[part]


def gather_kernel(got_ref, stats_ref, out_ref):
    total = got_ref[0].astype(F32)
    for p in range(1, got_ref.shape[0]):
        total = total + got_ref[p].astype(F32)
    count, span = total.shape
    for j in range(span // HD):
        out_ref[j * count : (j + 1) * count, :] = total[:, j * HD : (j + 1) * HD]
    out_ref[span // HD * count :, :] = stats_ref[...]


def spare_kernel(*refs):
    pass


def low_kernel(
    order, ids_hbm, block_ref, down_ref, far_hbm, out_ref, ids_ref, far_ref, low_ref, sems
):
    parts, per_dev, _ = out_ref.shape
    depth, columns = down_ref.shape
    ranks = columns // ADAPTERS
    pieces = sems.shape[0] - 1
    step = depth // pieces
    named = pltpu.make_async_copy(ids_hbm, ids_ref, sems.at[pieces])
    named.start()
    copies = [
        pltpu.make_async_copy(
            far_hbm.at[pl.ds(i * step, step)], far_ref.at[pl.ds(i * step, step)], sems.at[i]
        )
        for i in range(pieces)
    ]
    for copy in copies:
        copy.start()
    near = jnp.dot(block_ref[...], down_ref[...], preferred_element_type=F32)
    named.wait()
    names = across(one_hot_ids(ids_ref[...]), iota((ADAPTERS, 128), 0).astype(BF16))
    names = names.astype(jnp.int32)
    shift = order[0] * per_dev
    if shift:
        names = jnp.concatenate([names[shift:], names[:shift]], axis=0)
    lane = iota(names.shape, 1)
    spot = names + lane % 2 * ADAPTERS
    rank = lane % (2 * ranks)

    def take(values, half, low):
        for j in range(columns // 128):
            got = jnp.take_along_axis(values[:, j * 128 : (j + 1) * 128], spot, axis=1)
            low = jnp.where(rank // 2 == j + half * ranks // 2, got, low)
        return low

    low_ref[...] = take(near, 1, jnp.zeros(names.shape, F32))
    far = jnp.zeros(near.shape, F32)
    for i in range(pieces):
        copies[i].wait()
        part = slice(i * step, (i + 1) * step)
        far = far + jnp.dot(block_ref[:, part], far_ref[part, :], preferred_element_type=F32)
    low = take(far, 0, low_ref[...])
    high = low.astype(BF16).astype(F32)
    low = jnp.where(lane < 2 * ranks, high, low - high).astype(BF16)
    for p in range(parts):
        out_ref[p] = low[p * per_dev : (p + 1) * per_dev]


def total_kernel(ranks, got_ref, out_ref):
    total = got_ref[0].astype(F32)
    for p in range(1, got_ref.shape[0]):
        total = total + got_ref[p].astype(F32)
    total = total + pltpu.roll(total, 128 - 2 * ranks, 1)
    out_ref[: total.shape[0], :] = total.astype(BF16).astype(F32)


def merge_kernel(
    ranks, mine_ref, other_ref, stats_ref, base_ref, query_ref,
    kv_ref, out_ref, q_ref, wide_ref
):
    count, width = base_ref.shape
    heads = query_ref.shape[1] // HD
    halves = width // HD
    scale = HD ** (-0.5)
    lower = lax.axis_index("tp") == 0
    tile = halves * count
    span = 2 * ranks * tile
    query = query_ref[...].astype(F32)
    for h in range(heads):
        q_ref[pl.ds(h, count, stride=heads), :] = query[:, h * HD : (h + 1) * HD]
    low = jnp.where(lower, other_ref[:count, :], mine_ref[:count, :])
    low = jnp.concatenate([low] * halves, axis=0)
    base = base_ref[...].astype(F32)
    fresh = jnp.concatenate([base[:, j * HD : (j + 1) * HD] for j in range(halves)], axis=0)
    for r in range(2 * ranks):
        part = slice(r * tile, (r + 1) * tile)
        row = jnp.where(lower, mine_ref[part, :], other_ref[part, :])
        fresh = fresh + low[:, r : r + 1] * row
    fresh = fresh.astype(BF16).astype(F32)
    for j in range(halves):
        kv_ref[:, j * HD : (j + 1) * HD] = fresh[j * count : (j + 1) * count].astype(BF16)
    for b in range(count):
        part = slice(b * heads, (b + 1) * heads)
        far = slice(span + b * heads, span + (b + 1) * heads)
        key = fresh[b : b + 1]
        value = fresh[count + b : count + b + 1]
        own = jnp.sum(q_ref[part, :] * key, axis=1, keepdims=True) * scale
        acc = jnp.where(lower, stats_ref[part, :], other_ref[far, :])
        part = slice((count + b) * heads, (count + b + 1) * heads)
        far = slice(span + (count + b) * heads, span + (count + b + 1) * heads)
        both = jnp.where(lower, stats_ref[part, :], other_ref[far, :])
        top = both[:, :1]
        high = jnp.maximum(top, own)
        keep = jnp.exp(top - high)
        weight = jnp.exp(own - high)
        norm = 1.0 / (both[:, HD - 1 :] * keep + weight)
        part = slice(b * heads, (b + 1) * heads)
        wide_ref[part, :] = acc * (keep * norm) + (weight * norm) * value
    for h in range(heads):
        out_ref[:, h * HD : (h + 1) * HD] = wide_ref[pl.ds(h, count, stride=heads), :].astype(BF16)


def shards(
    hidden, adapter_ids, home_slot, lengths, query, kv_base, cache, adapter_down, adapter_up
):
    per_dev = hidden.shape[0]
    slots, ranks, width = adapter_up.shape
    parts = lax.axis_size("req")
    everyone = per_dev * parts
    block = hidden.shape[1] // parts
    heads = query.shape[1] // HD
    span = 2 * ranks * width
    center = (parts // 2 + 1) % parts
    order = [(center + p) % parts for p in range(parts)]
    depth = -(-slots // 8) * 8
    base = (lax.axis_index("req") * slots).astype(jnp.int32).reshape(1)
    core = lax.axis_index("tp").astype(jnp.int32)
    swap = [(0, 1), (1, 0)]
    stats_shape = jax.ShapeDtypeStruct((2 * per_dev * heads, HD), F32)
    trade_shape = jax.ShapeDtypeStruct((span // HD * per_dev + 2 * per_dev * heads, HD), F32)
    blocks_shape = jax.ShapeDtypeStruct((parts, per_dev, block), BF16)

    def pin(x):
        return pltpu.with_memory_space_constraint(x, pltpu.HBM)

    def exchange(x):
        return lax.all_to_all(
            x, "req", split_axis=0, concat_axis=0, tiled=True, axis_index_groups=[order]
        )

    ids = adapter_ids.reshape(1, everyone)
    blocks = pl.pallas_call(
        functools.partial(rotate_kernel, order),
        out_shape=blocks_shape,
        in_specs=[HBM],
        out_specs=VMEM,
        scratch_shapes=[pltpu.SemaphoreType.DMA((parts,))],
        cost_estimate=pl.CostEstimate(flops=0, transcendentals=0, bytes_accessed=1 << 23),
        compiler_params=PARAMS,
    )(pin(hidden))
    blocks, near_up, near_query, near_down = lax.optimization_barrier(
        (blocks, adapter_up, query, adapter_down)
    )
    far_up = lax.ppermute(near_up, "tp", swap)
    far_query = lax.ppermute(near_query, "tp", swap)
    far_down = lax.ppermute(near_down, "tp", swap)
    got = lax.cond(core == 1, exchange, lambda blocks: blocks, blocks)
    got, far_up, far_query = lax.optimization_barrier((got, far_up, far_query))

    def lower(far_up, far_query, lengths, ids, query, cache, home, up, base):
        packed = pl.pallas_call(
            functools.partial(pack_kernel, order),
            out_shape=jax.ShapeDtypeStruct((parts, per_dev, span), BF16),
            in_specs=[SMEM] + [HBM] * 3 + [VMEM],
            out_specs=VMEM,
            scratch_shapes=[
                pltpu.VMEM((1, everyone), jnp.int32),
                pltpu.VMEM((1, ADAPTERS), jnp.int32),
                pltpu.VMEM(up.shape, BF16),
                pltpu.VMEM((depth, span), F32),
                pltpu.VMEM((slots, ranks, width), F32),
                pltpu.SemaphoreType.DMA((3,)),
            ],
            compiler_params=PARAMS,
        )(base, pin(ids), pin(home), pin(up), far_up)
        got = exchange(packed)
        mine, far = pl.pallas_call(
            attend_kernel,
            out_shape=(stats_shape, stats_shape),
            in_specs=[SMEM, HBM, VMEM, HBM],
            out_specs=(VMEM, VMEM),
            scratch_shapes=[
                pltpu.VMEM(query.shape, BF16),
                pltpu.VMEM(cache.shape, BF16),
                pltpu.VMEM((2 * per_dev * heads, HD), F32),
                pltpu.SemaphoreType.DMA((2,)),
            ],
            compiler_params=PARAMS,
        )(lengths, pin(query), far_query, pin(cache))
        trade = pl.pallas_call(
            gather_kernel,
            out_shape=trade_shape,
            in_specs=[VMEM, VMEM],
            out_specs=VMEM,
            compiler_params=PARAMS,
        )(got, far)
        return mine, trade

    def upper(far_up, far_query, lengths, ids, query, cache, home, up, base):
        return pl.pallas_call(
            spare_kernel,
            out_shape=(stats_shape, trade_shape),
            in_specs=[],
            out_specs=(VMEM, VMEM),
            compiler_params=PARAMS,
        )()

    stats, trade = lax.cond(
        core == 1, upper, lower,
        far_up, far_query, lengths, ids, query, cache,
        home_slot.reshape(1, ADAPTERS), adapter_up, base,
    )
    far_down, trade = lax.optimization_barrier((far_down, trade))
    pieces = 4 if block % 64 == 0 else 1

    def upper_low(ids, got, down, far_down, trade):
        low = pl.pallas_call(
            functools.partial(low_kernel, order),
            out_shape=jax.ShapeDtypeStruct((parts, per_dev, 128), BF16),
            in_specs=[HBM, VMEM, VMEM, HBM],
            out_specs=VMEM,
            scratch_shapes=[
                pltpu.VMEM((1, everyone), jnp.int32),
                pltpu.VMEM(adapter_down.shape, BF16),
                pltpu.VMEM((everyone, 128), F32),
                pltpu.SemaphoreType.DMA((pieces + 1,)),
            ],
            compiler_params=PARAMS,
        )(pin(ids), got, down, pin(far_down))
        return pl.pallas_call(
            functools.partial(total_kernel, ranks),
            out_shape=trade_shape,
            in_specs=[VMEM],
            out_specs=VMEM,
            compiler_params=PARAMS,
        )(exchange(low))

    def lower_low(ids, got, down, far_down, trade):
        return trade

    mine = lax.cond(
        core == 1, upper_low, lower_low,
        ids, got.reshape(everyone, block), adapter_down, far_down, trade,
    )
    other = lax.ppermute(mine, "tp", swap)
    new_kv, attended = pl.pallas_call(
        functools.partial(merge_kernel, ranks),
        out_shape=(
            jax.ShapeDtypeStruct(kv_base.shape, BF16),
            jax.ShapeDtypeStruct(query.shape, BF16),
        ),
        in_specs=[VMEM] * 5,
        out_specs=(VMEM, VMEM),
        scratch_shapes=[
            pltpu.VMEM((per_dev * heads, HD), F32),
            pltpu.VMEM((per_dev * heads, HD), F32),
        ],
        compiler_params=PARAMS,
    )(mine, other, stats, kv_base, query)
    return (new_kv, attended)


def solution(mesh):
    placed = (
        P(("group", "req"), None),
        P("group"),
        P(),
        P(("group", "req")),
        P(("group", "req"), "tp"),
        P(("group", "req"), None),
        P(("group", "req"), None, None),
        P("req", "tp"),
        P("req", "tp", None),
    )
    return jax.shard_map(
        shards,
        mesh=mesh,
        in_specs=placed,
        out_specs=(P(("group", "req"), None), P(("group", "req"), "tp")),
        check_vma=False,
    )
```

```python
import functools

import jax
import jax.numpy as jnp
from jax import lax
from jax.experimental import pallas as pl
from jax.experimental.pallas import tpu as pltpu
from jax.sharding import PartitionSpec as P

HD = 128
ADAPTERS = 64
F32 = jnp.float32
BF16 = jnp.bfloat16
VMEM = pl.BlockSpec(memory_space=pltpu.VMEM)
SMEM = pl.BlockSpec(memory_space=pltpu.SMEM)
HBM = pl.BlockSpec(memory_space=pltpu.HBM)
PARAMS = pltpu.CompilerParams(vmem_limit_bytes=8 * 1024 * 1024)


def iota(shape, dim):
    return lax.broadcasted_iota(jnp.int32, shape, dim)


def one_hot_ids(ids):
    shape = (ADAPTERS, ids.shape[1])
    return (iota(shape, 0) == jnp.broadcast_to(ids, shape)).astype(BF16)


def across(a, b):
    return lax.dot_general(a, b, (((0,), (0,)), ((), ())), preferred_element_type=F32)


def rotate_kernel(order, hidden_ref, out_ref, sems):
    block = out_ref.shape[2]

    @pl.when(lax.axis_index("tp") == 1)
    def _():
        copies = [
            pltpu.make_async_copy(
                hidden_ref.at[:, pl.ds(q * block, block)], out_ref.at[p], sems.at[p]
            )
            for p, q in enumerate(order)
        ]
        for copy in copies:
            copy.start()
        for copy in copies:
            copy.wait()


def pack_kernel(
    order, base_ref, ids_hbm, home_hbm, up_hbm, far_ref, out_ref,
    ids_ref, home_ref, up_ref, flat_ref, wide_ref, sems
):
    pairs = ((ids_hbm, ids_ref), (home_hbm, home_ref), (up_hbm, up_ref))
    copies = [pltpu.make_async_copy(a, b, sems.at[i]) for i, (a, b) in enumerate(pairs)]
    for copy in copies:
        copy.start()
    for copy in copies:
        copy.wait()
    slots, ranks, width = up_ref.shape
    depth = flat_ref.shape[0]
    count = out_ref.shape[1]
    if depth > slots:
        flat_ref[...] = jnp.zeros_like(flat_ref)
    for half, ref in enumerate((up_ref, far_ref)):
        wide_ref[...] = ref[...].astype(F32)
        for r in range(ranks):
            at = (half * ranks + r) * width
            flat_ref[:slots, at : at + width] = wide_ref[:, r, :]
    shape = (depth, ADAPTERS)
    here = jnp.broadcast_to(home_ref[...], shape) - base_ref[0] == iota(shape, 0)
    held = here & (iota(shape, 0) < slots)
    match = jnp.dot(held.astype(BF16), one_hot_ids(ids_ref[...]), preferred_element_type=F32)
    rows = across(match.astype(BF16), flat_ref[...].astype(BF16)).astype(BF16)
    for p, q in enumerate(order):
        out_ref[p] = rows[q * count : (q + 1) * count]


def attend_kernel(
    lengths_ref, query_hbm, far_query_ref, cache_hbm, q_out_ref, mine_ref, far_ref, level_ref,
    query_ref, cache_ref, q_ref, sems
):
    pairs = ((query_hbm, query_ref), (cache_hbm, cache_ref))
    copies = [pltpu.make_async_copy(a, b, sems.at[i]) for i, (a, b) in enumerate(pairs)]
    for copy in copies:
        copy.start()
    for copy in copies:
        copy.wait()
    count = cache_ref.shape[0]
    heads = query_ref.shape[1] // HD
    scale = HD ** (-0.5)
    for half, ref in enumerate((query_ref, far_query_ref)):
        query = ref[...].astype(F32)
        for h in range(heads):
            q_ref[pl.ds(half * heads + h, count, stride=2 * heads), :] = query[
                :, h * HD : (h + 1) * HD
            ]
    for b in range(count):
        queries = q_ref[b * 2 * heads : (b + 1) * 2 * heads, :]
        scores = lax.dot_general(
            queries.astype(BF16),
            cache_ref[b, :, :HD],
            (((1,), (1,)), ((), ())),
            preferred_element_type=F32,
        )
        valid = iota(scores.shape, 1) < lengths_ref[b]
        scores = jnp.where(valid, scores * scale, -jnp.inf)
        top = jnp.max(scores, axis=1, keepdims=True)
        weights = jnp.exp(scores - top)
        total = jnp.sum(weights, axis=1, keepdims=True)
        acc = jnp.dot(weights.astype(BF16), cache_ref[b, :, HD:], preferred_element_type=F32)
        mean = acc / total
        level = jnp.broadcast_to(top + jnp.log(total), mean.shape)
        part = slice(b * heads, (b + 1) * heads)
        q_out_ref[part, :] = queries[:heads]
        mine_ref[part, :] = mean[:heads]
        far_ref[part, :] = mean[heads:]
        after = slice((count + b) * heads, (count + b + 1) * heads)
        mine_ref[after, :] = level[:heads]
        far_ref[after, :] = queries[heads:]
        level_ref[part, :] = level[heads:]


def thirds(values):
    lane = iota(values.shape, 1)
    high = values.astype(BF16).astype(F32)
    rest = values - high
    middle = rest.astype(BF16).astype(F32)
    low = rest - middle
    return jnp.where(lane < 32, high, jnp.where(lane < 64, middle, low)).astype(BF16)


def whole(values):
    values = values.astype(F32)
    return values[:, 0:1] + values[:, 32:33] + values[:, 64:65]


def gather_kernel(got_ref, stats_ref, level_ref, out_ref, wide_ref):
    total = got_ref[0].astype(F32)
    for p in range(1, got_ref.shape[0]):
        total = total + got_ref[p].astype(F32)
    count, span = total.shape
    rows = level_ref.shape[0]
    tall = span // HD * count
    for j in range(span // HD):
        wide_ref[j * count : (j + 1) * count, :] = total[:, j * HD : (j + 1) * HD]
    out_ref[:tall, :] = wide_ref[...].astype(BF16)
    out_ref[tall : tall + 2 * rows, :] = stats_ref[...].astype(BF16)
    out_ref[tall + 2 * rows :, :] = thirds(level_ref[...])


def spare_kernel(*refs):
    pass


def low_kernel(
    order, ids_hbm, block_ref, down_ref, far_hbm, out_ref, ids_ref, far_ref, low_ref, sems
):
    parts, per_dev, _ = out_ref.shape
    depth, columns = down_ref.shape
    ranks = columns // ADAPTERS
    pieces = sems.shape[0] - 1
    step = depth // pieces
    named = pltpu.make_async_copy(ids_hbm, ids_ref, sems.at[pieces])
    named.start()
    copies = [
        pltpu.make_async_copy(
            far_hbm.at[pl.ds(i * step, step)], far_ref.at[pl.ds(i * step, step)], sems.at[i]
        )
        for i in range(pieces)
    ]
    for copy in copies:
        copy.start()
    near = jnp.dot(block_ref[...], down_ref[...], preferred_element_type=F32)
    named.wait()
    names = across(one_hot_ids(ids_ref[...]), iota((ADAPTERS, 128), 0).astype(BF16))
    names = names.astype(jnp.int32)
    shift = order[0] * per_dev
    if shift:
        names = jnp.concatenate([names[shift:], names[:shift]], axis=0)
    lane = iota(names.shape, 1)
    spot = names + lane % 2 * ADAPTERS
    rank = lane % (2 * ranks)

    def take(values, half, low):
        for j in range(columns // 128):
            got = jnp.take_along_axis(values[:, j * 128 : (j + 1) * 128], spot, axis=1)
            low = jnp.where(rank // 2 == j + half * ranks // 2, got, low)
        return low

    low_ref[...] = take(near, 1, jnp.zeros(names.shape, F32))
    far = jnp.zeros(near.shape, F32)
    for i in range(pieces):
        copies[i].wait()
        part = slice(i * step, (i + 1) * step)
        far = far + jnp.dot(block_ref[:, part], far_ref[part, :], preferred_element_type=F32)
    low = take(far, 0, low_ref[...])
    high = low.astype(BF16).astype(F32)
    low = jnp.where(lane < 2 * ranks, high, low - high).astype(BF16)
    for p in range(parts):
        out_ref[p] = low[p * per_dev : (p + 1) * per_dev]


def total_kernel(ranks, got_ref, out_ref):
    total = got_ref[0].astype(F32)
    for p in range(1, got_ref.shape[0]):
        total = total + got_ref[p].astype(F32)
    total = total + pltpu.roll(total, 128 - 2 * ranks, 1)
    out_ref[:16, :] = jnp.concatenate([total] * (16 // total.shape[0]), axis=0).astype(BF16)


def merge_kernel(
    ranks, mine_ref, other_ref, q_ref, stats_ref, base_ref, kv_ref, out_ref, wide_ref
):
    count, width = base_ref.shape
    rows = q_ref.shape[0]
    heads = rows // count
    halves = width // HD
    tile = halves * count
    span = 2 * ranks * tile
    lower = lax.axis_index("tp") == 0
    base = base_ref[...].astype(F32)
    fresh = jnp.concatenate([base[:, j * HD : (j + 1) * HD] for j in range(halves)], axis=0)
    low = jnp.where(lower, other_ref[:16, :], mine_ref[:16, :]).astype(F32)[:tile]
    for r in range(0, 2 * ranks, 16 // tile):
        part = slice(r * tile, r * tile + 16)
        pair = jnp.where(lower, mine_ref[part, :], other_ref[part, :]).astype(F32)
        for i in range(16 // tile):
            fresh = fresh + low[:, r + i : r + i + 1] * pair[i * tile : (i + 1) * tile]
    fresh = fresh.astype(BF16).astype(F32)
    for j in range(halves):
        kv_ref[:, j * HD : (j + 1) * HD] = fresh[j * count : (j + 1) * count].astype(BF16)
    far = other_ref[span:, :].astype(F32)
    mean = jnp.where(lower, stats_ref[:rows, :], far[:rows])
    query = jnp.where(lower, q_ref[...], far[rows : 2 * rows])
    level = jnp.where(lower, stats_ref[rows:, :1], whole(far[2 * rows :]))
    spread = [
        jnp.concatenate(
            [
                jnp.broadcast_to(fresh[j * count + b : j * count + b + 1], (heads, HD))
                for b in range(count)
            ],
            axis=0,
        )
        for j in range(halves)
    ]
    own = jnp.sum(query * spread[0], axis=1, keepdims=True) * HD ** (-0.5)
    share = 1.0 / (1.0 + jnp.exp(level - own))
    wide_ref[...] = mean + share * (spread[1] - mean)
    for h in range(heads):
        out_ref[:, h * HD : (h + 1) * HD] = wide_ref[pl.ds(h, count, stride=heads), :].astype(BF16)


def shards(
    hidden, adapter_ids, home_slot, lengths, query, kv_base, cache, adapter_down, adapter_up
):
    per_dev = hidden.shape[0]
    slots, ranks, width = adapter_up.shape
    parts = lax.axis_size("req")
    everyone = per_dev * parts
    block = hidden.shape[1] // parts
    heads = query.shape[1] // HD
    span = 2 * ranks * width
    center = (parts // 2 + 1) % parts
    order = [(center + p) % parts for p in range(parts)]
    depth = -(-slots // 8) * 8
    base = (lax.axis_index("req") * slots).astype(jnp.int32).reshape(1)
    core = lax.axis_index("tp").astype(jnp.int32)
    swap = [(0, 1), (1, 0)]
    stats_shape = jax.ShapeDtypeStruct((2 * per_dev * heads, HD), F32)
    heads_shape = jax.ShapeDtypeStruct((per_dev * heads, HD), F32)
    trade_shape = jax.ShapeDtypeStruct((span // HD * per_dev + 3 * per_dev * heads, HD), BF16)
    blocks_shape = jax.ShapeDtypeStruct((parts, per_dev, block), BF16)

    def pin(x):
        return pltpu.with_memory_space_constraint(x, pltpu.HBM)

    def exchange(x):
        return lax.all_to_all(
            x, "req", split_axis=0, concat_axis=0, tiled=True, axis_index_groups=[order]
        )

    ids = adapter_ids.reshape(1, everyone)
    blocks = pl.pallas_call(
        functools.partial(rotate_kernel, order),
        out_shape=blocks_shape,
        in_specs=[HBM],
        out_specs=VMEM,
        scratch_shapes=[pltpu.SemaphoreType.DMA((parts,))],
        cost_estimate=pl.CostEstimate(flops=0, transcendentals=0, bytes_accessed=1 << 23),
        compiler_params=PARAMS,
    )(pin(hidden))
    blocks, near_up, near_query, near_down = lax.optimization_barrier(
        (blocks, adapter_up, query, adapter_down)
    )
    far_up = lax.ppermute(near_up, "tp", swap)
    far_query = lax.ppermute(near_query, "tp", swap)
    far_down = lax.ppermute(near_down, "tp", swap)
    got = lax.cond(core == 1, exchange, lambda blocks: blocks, blocks)
    got, far_up, far_query = lax.optimization_barrier((got, far_up, far_query))

    def lower(far_up, far_query, lengths, ids, query, cache, home, up, base):
        packed = pl.pallas_call(
            functools.partial(pack_kernel, order),
            out_shape=jax.ShapeDtypeStruct((parts, per_dev, span), BF16),
            in_specs=[SMEM] + [HBM] * 3 + [VMEM],
            out_specs=VMEM,
            scratch_shapes=[
                pltpu.VMEM((1, everyone), jnp.int32),
                pltpu.VMEM((1, ADAPTERS), jnp.int32),
                pltpu.VMEM(up.shape, BF16),
                pltpu.VMEM((depth, span), F32),
                pltpu.VMEM((slots, ranks, width), F32),
                pltpu.SemaphoreType.DMA((3,)),
            ],
            compiler_params=PARAMS,
        )(base, pin(ids), pin(home), pin(up), far_up)
        got = exchange(packed)
        near_q, mine, far, level = pl.pallas_call(
            attend_kernel,
            out_shape=(heads_shape, stats_shape, stats_shape, heads_shape),
            in_specs=[SMEM, HBM, VMEM, HBM],
            out_specs=(VMEM,) * 4,
            scratch_shapes=[
                pltpu.VMEM(query.shape, BF16),
                pltpu.VMEM(cache.shape, BF16),
                pltpu.VMEM((2 * per_dev * heads, HD), F32),
                pltpu.SemaphoreType.DMA((2,)),
            ],
            compiler_params=PARAMS,
        )(lengths, pin(query), far_query, pin(cache))
        trade = pl.pallas_call(
            gather_kernel,
            out_shape=trade_shape,
            in_specs=[VMEM] * 3,
            out_specs=VMEM,
            scratch_shapes=[pltpu.VMEM((span // HD * per_dev, HD), F32)],
            compiler_params=PARAMS,
        )(got, far, level)
        return near_q, mine, trade

    def upper(far_up, far_query, lengths, ids, query, cache, home, up, base):
        return pl.pallas_call(
            spare_kernel,
            out_shape=(heads_shape, stats_shape, trade_shape),
            in_specs=[],
            out_specs=(VMEM,) * 3,
            compiler_params=PARAMS,
        )()

    near_q, stats, trade = lax.cond(
        core == 1, upper, lower,
        far_up, far_query, lengths, ids, query, cache,
        home_slot.reshape(1, ADAPTERS), adapter_up, base,
    )
    far_down, trade = lax.optimization_barrier((far_down, trade))
    pieces = 4 if block % 64 == 0 else 1

    def upper_low(ids, got, down, far_down, trade):
        low = pl.pallas_call(
            functools.partial(low_kernel, order),
            out_shape=jax.ShapeDtypeStruct((parts, per_dev, 128), BF16),
            in_specs=[HBM, VMEM, VMEM, HBM],
            out_specs=VMEM,
            scratch_shapes=[
                pltpu.VMEM((1, everyone), jnp.int32),
                pltpu.VMEM(adapter_down.shape, BF16),
                pltpu.VMEM((everyone, 128), F32),
                pltpu.SemaphoreType.DMA((pieces + 1,)),
            ],
            compiler_params=PARAMS,
        )(pin(ids), got, down, pin(far_down))
        return pl.pallas_call(
            functools.partial(total_kernel, ranks),
            out_shape=trade_shape,
            in_specs=[VMEM],
            out_specs=VMEM,
            compiler_params=PARAMS,
        )(exchange(low))

    def lower_low(ids, got, down, far_down, trade):
        return trade

    mine = lax.cond(
        core == 1, upper_low, lower_low,
        ids, got.reshape(everyone, block), adapter_down, far_down, trade,
    )
    other = lax.ppermute(mine, "tp", swap)
    new_kv, attended = pl.pallas_call(
        functools.partial(merge_kernel, ranks),
        out_shape=(
            jax.ShapeDtypeStruct(kv_base.shape, BF16),
            jax.ShapeDtypeStruct(query.shape, BF16),
        ),
        in_specs=[VMEM] * 5,
        out_specs=(VMEM, VMEM),
        scratch_shapes=[pltpu.VMEM((per_dev * heads, HD), F32)],
        compiler_params=PARAMS,
    )(mine, other, near_q, stats, kv_base)
    return (new_kv, attended)


def solution(mesh):
    placed = (
        P(("group", "req"), None),
        P("group"),
        P(),
        P(("group", "req")),
        P(("group", "req"), "tp"),
        P(("group", "req"), None),
        P(("group", "req"), None, None),
        P("req", "tp"),
        P("req", "tp", None),
    )
    return jax.shard_map(
        shards,
        mesh=mesh,
        in_specs=placed,
        out_specs=(P(("group", "req"), None), P(("group", "req"), "tp")),
        check_vma=False,
    )
```

```python
import functools

import jax
import jax.numpy as jnp
from jax import lax
from jax.experimental import pallas as pl
from jax.experimental.pallas import tpu as pltpu
from jax.sharding import PartitionSpec as P

HD = 128
ADAPTERS = 64
F32 = jnp.float32
BF16 = jnp.bfloat16
VMEM = pl.BlockSpec(memory_space=pltpu.VMEM)
SMEM = pl.BlockSpec(memory_space=pltpu.SMEM)
HBM = pl.BlockSpec(memory_space=pltpu.HBM)
PARAMS = pltpu.CompilerParams(vmem_limit_bytes=8 * 1024 * 1024)


def iota(shape, dim):
    return lax.broadcasted_iota(jnp.int32, shape, dim)


def one_hot_ids(ids):
    shape = (ADAPTERS, ids.shape[1])
    return (iota(shape, 0) == jnp.broadcast_to(ids, shape)).astype(BF16)


def across(a, b):
    return lax.dot_general(a, b, (((0,), (0,)), ((), ())), preferred_element_type=F32)


def start_kernel(
    hidden_ref, ids_hbm, home_hbm, up_hbm, out_ref, ids_ref, home_ref, up_ref, sems
):
    parts, _, block = hidden_ref.shape
    center = (parts // 2 + 1) % parts

    @pl.when(lax.axis_index("tp") == 1)
    def _():
        copies = [
            pltpu.make_async_copy(
                hidden_ref.at[pl.ds(center, parts - center)],
                out_ref.at[pl.ds(0, parts - center), :, pl.ds(0, block)],
                sems.at[0],
            ),
            pltpu.make_async_copy(
                hidden_ref.at[pl.ds(0, center)],
                out_ref.at[pl.ds(parts - center, center), :, pl.ds(0, block)],
                sems.at[1],
            ),
            pltpu.make_async_copy(ids_hbm, ids_ref, sems.at[2]),
            pltpu.make_async_copy(home_hbm, home_ref, sems.at[3]),
            pltpu.make_async_copy(up_hbm, up_ref, sems.at[4]),
        ]
        for copy in copies:
            copy.start()
        for copy in copies:
            copy.wait()


def needed_rows(ids, home, up_ref, flat_ref, wide_ref):
    slots, ranks, width = up_ref.shape
    depth = flat_ref.shape[0]
    if depth > slots:
        flat_ref[...] = jnp.zeros_like(flat_ref)
    wide_ref[...] = up_ref[...].astype(F32)
    for r in range(ranks):
        flat_ref[:slots, r * width : (r + 1) * width] = wide_ref[:, r, :]
    shape = (depth, ADAPTERS)
    base = lax.axis_index("req").astype(jnp.int32) * slots
    here = jnp.broadcast_to(home, shape) - base == iota(shape, 0)
    held = here & (iota(shape, 0) < slots)
    match = jnp.dot(held.astype(BF16), one_hot_ids(ids), preferred_element_type=F32)
    return across(match.astype(BF16), flat_ref[...].astype(BF16)).astype(BF16)


def pack_kernel(
    order, blocks_ref, ids_hbm, home_hbm, up_hbm, cache_hbm, down_hbm, out_ref,
    ids_ref, home_ref, up_ref, flat_ref, wide_ref, sems
):
    count = out_ref.shape[1]
    span = flat_ref.shape[1]
    lower = lax.axis_index("tp") == 0

    @pl.when(lower)
    def _():
        pairs = ((ids_hbm, ids_ref), (home_hbm, home_ref), (up_hbm, up_ref))
        copies = [pltpu.make_async_copy(a, b, sems.at[i]) for i, (a, b) in enumerate(pairs)]
        for copy in copies:
            copy.start()
        for copy in copies:
            copy.wait()
        rows = needed_rows(ids_ref[...], home_ref[...], up_ref, flat_ref, wide_ref)
        for p, q in enumerate(order):
            out_ref[p, :, :span] = rows[q * count : (q + 1) * count]

    @pl.when(jnp.logical_not(lower))
    def _():
        out_ref[...] = blocks_ref[...]


def low_kernel(
    order, ids_ref, home_ref, up_ref, got_ref, down_ref, far_ref, out_ref, flat_ref, wide_ref
):
    parts, per_dev, _ = out_ref.shape
    block, columns = down_ref.shape
    ranks = columns // ADAPTERS
    span = flat_ref.shape[1]

    @pl.when(lax.axis_index("tp") == 1)
    def _():
        pieces = [got_ref[p].astype(F32)[:, :block] for p in range(parts)]
        blocks = jnp.concatenate(pieces, axis=0).astype(BF16)
        names = across(one_hot_ids(ids_ref[...]), iota((ADAPTERS, 128), 0).astype(BF16))
        names = names.astype(jnp.int32)
        shift = order[0] * per_dev
        if shift:
            names = jnp.concatenate([names[shift:], names[:shift]], axis=0)
        lane = iota(names.shape, 1)
        spot = names + lane % 2 * ADAPTERS
        rank = lane % (2 * ranks)
        low = jnp.zeros(names.shape, F32)
        for half, ref in enumerate((far_ref, down_ref)):
            values = jnp.dot(blocks, ref[...], preferred_element_type=F32)
            for j in range(columns // 128):
                got = jnp.take_along_axis(values[:, j * 128 : (j + 1) * 128], spot, axis=1)
                low = jnp.where(rank // 2 == j + half * ranks // 2, got, low)
        high = low.astype(BF16).astype(F32)
        low = jnp.where(lane < 2 * ranks, high, low - high).astype(BF16)
        rows = needed_rows(ids_ref[...], home_ref[...], up_ref, flat_ref, wide_ref)
        for p, q in enumerate(order):
            out_ref[p, :, :span] = rows[q * per_dev : (q + 1) * per_dev]
            out_ref[p, :, span:] = low[p * per_dev : (p + 1) * per_dev]


def fold_kernel(ranks, span, got_ref, out_ref, wide_ref):
    total = got_ref[0].astype(F32)
    for p in range(1, got_ref.shape[0]):
        total = total + got_ref[p].astype(F32)
    count = total.shape[0]
    tall = span // HD * count
    for j in range(span // HD):
        wide_ref[j * count : (j + 1) * count, :] = total[:, j * HD : (j + 1) * HD]
    out_ref[:tall, :] = wide_ref[...].astype(BF16)
    if total.shape[1] == span + 128:
        low = total[:, span:]
        low = low + pltpu.roll(low, 128 - 2 * ranks, 1)
        out_ref[tall:, :] = jnp.concatenate([low] * (16 // count), axis=0).astype(BF16)


def attend_kernel(lengths_ref, query_ref, cache_ref, q_ref, stats_ref):
    count = cache_ref.shape[0]
    heads = query_ref.shape[1] // HD
    scale = HD ** (-0.5)
    query = query_ref[...].astype(F32)
    lengths = lengths_ref[...]
    for h in range(heads):
        q_ref[pl.ds(h, count, stride=heads), :] = query[:, h * HD : (h + 1) * HD]
    for b in range(count):
        part = slice(b * heads, (b + 1) * heads)
        scores = lax.dot_general(
            q_ref[part, :].astype(BF16),
            cache_ref[b, :, :HD],
            (((1,), (1,)), ((), ())),
            preferred_element_type=F32,
        )
        valid = iota(scores.shape, 1) < lengths[:, b : b + 1]
        scores = jnp.where(valid, scores * scale, -jnp.inf)
        top = jnp.max(scores, axis=1, keepdims=True)
        weights = jnp.exp(scores - top)
        total = jnp.sum(weights, axis=1, keepdims=True)
        acc = jnp.dot(weights.astype(BF16), cache_ref[b, :, HD:], preferred_element_type=F32)
        stats_ref[part, :] = acc / total
        after = slice((count + b) * heads, (count + b + 1) * heads)
        stats_ref[after, :] = jnp.broadcast_to(top + jnp.log(total), acc.shape)


def merge_kernel(
    ranks, mine_ref, other_ref, q_ref, stats_ref, base_ref, kv_ref, out_ref, wide_ref
):
    count, width = base_ref.shape
    rows = q_ref.shape[0]
    heads = rows // count
    halves = width // HD
    tile = halves * count
    span = ranks * tile
    lower = lax.axis_index("tp") == 0
    base = base_ref[...].astype(F32)
    fresh = jnp.concatenate([base[:, j * HD : (j + 1) * HD] for j in range(halves)], axis=0)
    low = jnp.where(lower, other_ref[span:, :], mine_ref[span:, :]).astype(F32)[:tile]
    for r in range(0, ranks, 16 // tile):
        part = slice(r * tile, r * tile + 16)
        mine = mine_ref[part, :]
        other = other_ref[part, :]
        for half, pair in ((0, jnp.where(lower, mine, other)), (1, jnp.where(lower, other, mine))):
            pair = pair.astype(F32)
            for i in range(16 // tile):
                at = half * ranks + r + i
                fresh = fresh + low[:, at : at + 1] * pair[i * tile : (i + 1) * tile]
    fresh = fresh.astype(BF16).astype(F32)
    for j in range(halves):
        kv_ref[:, j * HD : (j + 1) * HD] = fresh[j * count : (j + 1) * count].astype(BF16)
    mean = stats_ref[:rows, :]
    level = stats_ref[rows:, :1]
    spread = [
        jnp.concatenate(
            [
                jnp.broadcast_to(fresh[j * count + b : j * count + b + 1], (heads, HD))
                for b in range(count)
            ],
            axis=0,
        )
        for j in range(halves)
    ]
    own = jnp.sum(q_ref[...] * spread[0], axis=1, keepdims=True) * HD ** (-0.5)
    share = 1.0 / (1.0 + jnp.exp(level - own))
    wide_ref[...] = mean + share * (spread[1] - mean)
    for h in range(heads):
        out_ref[:, h * HD : (h + 1) * HD] = wide_ref[pl.ds(h, count, stride=heads), :].astype(BF16)


def shards(
    hidden, adapter_ids, home_slot, lengths, query, kv_base, cache, adapter_down, adapter_up
):
    per_dev = hidden.shape[0]
    slots, ranks, width = adapter_up.shape
    parts = lax.axis_size("req")
    everyone = per_dev * parts
    block = hidden.shape[1] // parts
    heads = query.shape[1] // HD
    span = ranks * width
    wide = max(block, span)
    center = (parts // 2 + 1) % parts
    order = [(center + p) % parts for p in range(parts)]
    depth = -(-slots // 8) * 8
    core = lax.axis_index("tp").astype(jnp.int32)
    swap = [(0, 1), (1, 0)]
    blocks_shape = jax.ShapeDtypeStruct((parts, per_dev, wide), BF16)
    tall = span // HD * per_dev
    trade_shape = jax.ShapeDtypeStruct((tall + 16, HD), BF16)

    def pin(x):
        return pltpu.with_memory_space_constraint(x, pltpu.HBM)

    def exchange(x):
        return lax.all_to_all(
            x, "req", split_axis=0, concat_axis=0, tiled=True, axis_index_groups=[order]
        )

    ids = adapter_ids.reshape(1, everyone)
    home = home_slot.reshape(1, ADAPTERS)
    like = lambda x: jax.ShapeDtypeStruct(x.shape, x.dtype)
    blocks, near_ids, near_home, near_up = pl.pallas_call(
        start_kernel,
        out_shape=(blocks_shape, like(ids), like(home), like(adapter_up)),
        in_specs=[HBM] * 4,
        out_specs=(VMEM,) * 4,
        scratch_shapes=[pltpu.SemaphoreType.DMA((5,))],
        compiler_params=PARAMS,
    )(
        pin(jnp.swapaxes(hidden.reshape(per_dev, parts, block), 0, 1)),
        pin(ids),
        pin(home),
        pin(adapter_up),
    )
    blocks, near_down, lower = lax.optimization_barrier((blocks, adapter_down, core == 0))
    far_down = lax.ppermute(near_down, "tp", swap)
    blocks = pl.pallas_call(
        functools.partial(pack_kernel, order),
        out_shape=blocks_shape,
        in_specs=[VMEM] + [HBM] * 5,
        out_specs=VMEM,
        scratch_shapes=[
            pltpu.VMEM(ids.shape, ids.dtype),
            pltpu.VMEM(home.shape, home.dtype),
            pltpu.VMEM(adapter_up.shape, BF16),
            pltpu.VMEM((depth, span), F32),
            pltpu.VMEM((slots, ranks, width), F32),
            pltpu.SemaphoreType.DMA((3,)),
        ],
        compiler_params=PARAMS,
    )(blocks, pin(ids), pin(home), pin(adapter_up), pin(cache), pin(near_down))
    got = exchange(blocks)
    packed = pl.pallas_call(
        functools.partial(low_kernel, order),
        out_shape=jax.ShapeDtypeStruct((parts, per_dev, span + 128), BF16),
        in_specs=[VMEM] * 6,
        out_specs=VMEM,
        scratch_shapes=[
            pltpu.VMEM((depth, span), F32),
            pltpu.VMEM((slots, ranks, width), F32),
        ],
        compiler_params=PARAMS,
    )(near_ids, near_home, near_up, got, near_down, far_down)

    packed, got, lower = lax.optimization_barrier((packed, got, lower))

    def fold(x):
        return pl.pallas_call(
            functools.partial(fold_kernel, ranks, span),
            out_shape=trade_shape,
            in_specs=[VMEM],
            out_specs=VMEM,
            scratch_shapes=[pltpu.VMEM((tall, HD), F32)],
            compiler_params=PARAMS,
        )(x)

    mine = lax.cond(
        lower,
        lambda packed, got: fold(got[:, :, :span]),
        lambda packed, got: fold(exchange(packed)),
        packed, got,
    )
    mine, lengths, query, cache = lax.optimization_barrier((mine, lengths, query, cache))
    other = lax.ppermute(mine, "tp", swap)
    q_rows, stats = pl.pallas_call(
        attend_kernel,
        out_shape=(
            jax.ShapeDtypeStruct((per_dev * heads, HD), F32),
            jax.ShapeDtypeStruct((2 * per_dev * heads, HD), F32),
        ),
        in_specs=[VMEM] * 3,
        out_specs=(VMEM, VMEM),
        cost_estimate=pl.CostEstimate(flops=0, transcendentals=0, bytes_accessed=1 << 22),
        compiler_params=PARAMS,
    )(lengths.reshape(1, per_dev), query, cache)
    new_kv, attended = pl.pallas_call(
        functools.partial(merge_kernel, ranks),
        out_shape=(
            jax.ShapeDtypeStruct(kv_base.shape, BF16),
            jax.ShapeDtypeStruct(query.shape, BF16),
        ),
        in_specs=[VMEM] * 5,
        out_specs=(VMEM, VMEM),
        scratch_shapes=[pltpu.VMEM((per_dev * heads, HD), F32)],
        compiler_params=PARAMS,
    )(mine, other, q_rows, stats, kv_base)
    return (new_kv, attended)


def solution(mesh):
    placed = (
        P(("group", "req"), None),
        P("group"),
        P(),
        P(("group", "req")),
        P(("group", "req"), "tp"),
        P(("group", "req"), None),
        P(("group", "req"), None, None),
        P("req", "tp"),
        P("req", "tp", None),
    )
    return jax.shard_map(
        shards,
        mesh=mesh,
        in_specs=placed,
        out_specs=(P(("group", "req"), None), P(("group", "req"), "tp")),
        check_vma=False,
    )
```

```python
import functools

import jax
import jax.numpy as jnp
from jax import lax
from jax.experimental import pallas as pl
from jax.experimental.pallas import tpu as pltpu
from jax.sharding import PartitionSpec as P

HD = 128
ADAPTERS = 64
F32 = jnp.float32
BF16 = jnp.bfloat16
VMEM = pl.BlockSpec(memory_space=pltpu.VMEM)
SMEM = pl.BlockSpec(memory_space=pltpu.SMEM)
HBM = pl.BlockSpec(memory_space=pltpu.HBM)
PARAMS = pltpu.CompilerParams(vmem_limit_bytes=8 * 1024 * 1024)


def iota(shape, dim):
    return lax.broadcasted_iota(jnp.int32, shape, dim)


def one_hot_ids(ids):
    shape = (ADAPTERS, ids.shape[1])
    return (iota(shape, 0) == jnp.broadcast_to(ids, shape)).astype(BF16)


def across(a, b):
    return lax.dot_general(a, b, (((0,), (0,)), ((), ())), preferred_element_type=F32)


def start_kernel(
    hidden_ref, ids_hbm, home_hbm, up_hbm, out_ref, ids_ref, home_ref, up_ref, sems
):
    parts, _, block = hidden_ref.shape
    center = (parts // 2 + 1) % parts

    @pl.when(lax.axis_index("tp") == 1)
    def _():
        copies = [
            pltpu.make_async_copy(
                hidden_ref.at[pl.ds(center, parts - center)],
                out_ref.at[pl.ds(0, parts - center), :, pl.ds(0, block)],
                sems.at[0],
            ),
            pltpu.make_async_copy(
                hidden_ref.at[pl.ds(0, center)],
                out_ref.at[pl.ds(parts - center, center), :, pl.ds(0, block)],
                sems.at[1],
            ),
            pltpu.make_async_copy(ids_hbm, ids_ref, sems.at[2]),
            pltpu.make_async_copy(home_hbm, home_ref, sems.at[3]),
            pltpu.make_async_copy(up_hbm, up_ref, sems.at[4]),
        ]
        for copy in copies:
            copy.start()
        for copy in copies:
            copy.wait()


def needed_rows(ids, home, up_ref, flat_ref, wide_ref):
    slots, ranks, width = up_ref.shape
    depth = flat_ref.shape[0]
    if depth > slots:
        flat_ref[...] = jnp.zeros_like(flat_ref)
    wide_ref[...] = up_ref[...].astype(F32)
    for r in range(ranks):
        flat_ref[:slots, r * width : (r + 1) * width] = wide_ref[:, r, :]
    shape = (depth, ADAPTERS)
    base = lax.axis_index("req").astype(jnp.int32) * slots
    here = jnp.broadcast_to(home, shape) - base == iota(shape, 0)
    held = here & (iota(shape, 0) < slots)
    match = jnp.dot(held.astype(BF16), one_hot_ids(ids), preferred_element_type=F32)
    return across(match.astype(BF16), flat_ref[...].astype(BF16)).astype(BF16)


def pack_kernel(
    order, blocks_ref, ids_hbm, home_hbm, up_hbm, cache_hbm, down_hbm, *rest
):
    pack(order, blocks_ref, ids_hbm, home_hbm, up_hbm, *rest[2:])


def pack(
    order, blocks_ref, ids_hbm, home_hbm, up_hbm, out_ref,
    ids_ref, home_ref, up_ref, flat_ref, wide_ref, sems
):
    count = out_ref.shape[1]
    span = flat_ref.shape[1]
    lower = lax.axis_index("tp") == 0

    @pl.when(lower)
    def _():
        pairs = ((ids_hbm, ids_ref), (home_hbm, home_ref), (up_hbm, up_ref))
        copies = [pltpu.make_async_copy(a, b, sems.at[i]) for i, (a, b) in enumerate(pairs)]
        for copy in copies:
            copy.start()
        for copy in copies:
            copy.wait()
        rows = needed_rows(ids_ref[...], home_ref[...], up_ref, flat_ref, wide_ref)
        for p, q in enumerate(order):
            out_ref[p, :, :span] = rows[q * count : (q + 1) * count]

    @pl.when(jnp.logical_not(lower))
    def _():
        out_ref[...] = blocks_ref[...]


def low_kernel(
    order, ids_ref, home_ref, up_ref, got_ref, down_ref, far_ref, out_ref, flat_ref, wide_ref
):
    parts, per_dev, _ = out_ref.shape
    block, columns = down_ref.shape
    ranks = columns // ADAPTERS
    span = flat_ref.shape[1]

    @pl.when(lax.axis_index("tp") == 1)
    def _():
        pieces = [got_ref[p].astype(F32)[:, :block] for p in range(parts)]
        blocks = jnp.concatenate(pieces, axis=0).astype(BF16)
        names = across(one_hot_ids(ids_ref[...]), iota((ADAPTERS, 128), 0).astype(BF16))
        names = names.astype(jnp.int32)
        shift = order[0] * per_dev
        if shift:
            names = jnp.concatenate([names[shift:], names[:shift]], axis=0)
        lane = iota(names.shape, 1)
        spot = names + lane % 2 * ADAPTERS
        rank = lane % (2 * ranks)
        low = jnp.zeros(names.shape, F32)
        for half, ref in enumerate((far_ref, down_ref)):
            for j in range(columns // 128):
                values = jnp.dot(
                    blocks, ref[:, j * 128 : (j + 1) * 128], preferred_element_type=F32
                )
                got = jnp.take_along_axis(values, spot, axis=1)
                low = jnp.where(rank // 2 == j + half * ranks // 2, got, low)
        high = low.astype(BF16).astype(F32)
        low = jnp.where(lane < 2 * ranks, high, low - high).astype(BF16)
        rows = needed_rows(ids_ref[...], home_ref[...], up_ref, flat_ref, wide_ref)
        for p, q in enumerate(order):
            out_ref[p, :, :span] = rows[q * per_dev : (q + 1) * per_dev]
            out_ref[p, :, span:] = low[p * per_dev : (p + 1) * per_dev]


def fold_kernel(ranks, span, got_ref, out_ref, wide_ref):
    total = got_ref[0].astype(F32)
    for p in range(1, got_ref.shape[0]):
        total = total + got_ref[p].astype(F32)
    count = total.shape[0]
    tall = span // HD * count
    for j in range(span // HD):
        wide_ref[j * count : (j + 1) * count, :] = total[:, j * HD : (j + 1) * HD]
    out_ref[:tall, :] = wide_ref[...].astype(BF16)
    if total.shape[1] == span + 128:
        low = total[:, span:]
        low = low + pltpu.roll(low, 128 - 2 * ranks, 1)
        out_ref[tall:, :] = jnp.concatenate([low] * (16 // count), axis=0).astype(BF16)


def attend_kernel(lengths_ref, query_ref, cache_ref, q_ref, stats_ref):
    count = cache_ref.shape[0]
    heads = query_ref.shape[1] // HD
    scale = HD ** (-0.5)
    query = query_ref[...].astype(F32)
    lengths = lengths_ref[...]
    for h in range(heads):
        q_ref[pl.ds(h, count, stride=heads), :] = query[:, h * HD : (h + 1) * HD]
    for b in range(count):
        part = slice(b * heads, (b + 1) * heads)
        scores = lax.dot_general(
            q_ref[part, :].astype(BF16),
            cache_ref[b, :, :HD],
            (((1,), (1,)), ((), ())),
            preferred_element_type=F32,
        )
        valid = iota(scores.shape, 1) < lengths[:, b : b + 1]
        scores = jnp.where(valid, scores * scale, -jnp.inf)
        top = jnp.max(scores, axis=1, keepdims=True)
        weights = jnp.exp(scores - top)
        total = jnp.sum(weights, axis=1, keepdims=True)
        acc = jnp.dot(weights.astype(BF16), cache_ref[b, :, HD:], preferred_element_type=F32)
        stats_ref[part, :] = acc / total
        after = slice((count + b) * heads, (count + b + 1) * heads)
        stats_ref[after, :] = jnp.broadcast_to(top + jnp.log(total), acc.shape)


def merge_kernel(
    ranks, mine_ref, other_ref, q_ref, stats_ref, base_ref, kv_ref, out_ref, wide_ref
):
    count, width = base_ref.shape
    rows = q_ref.shape[0]
    heads = rows // count
    halves = width // HD
    tile = halves * count
    span = ranks * tile
    lower = lax.axis_index("tp") == 0
    base = base_ref[...].astype(F32)
    fresh = jnp.concatenate([base[:, j * HD : (j + 1) * HD] for j in range(halves)], axis=0)
    low = jnp.where(lower, other_ref[span:, :], mine_ref[span:, :]).astype(F32)[:tile]
    for r in range(0, ranks, 16 // tile):
        part = slice(r * tile, r * tile + 16)
        mine = mine_ref[part, :]
        other = other_ref[part, :]
        for half, pair in ((0, jnp.where(lower, mine, other)), (1, jnp.where(lower, other, mine))):
            pair = pair.astype(F32)
            for i in range(16 // tile):
                at = half * ranks + r + i
                fresh = fresh + low[:, at : at + 1] * pair[i * tile : (i + 1) * tile]
    fresh = fresh.astype(BF16).astype(F32)
    for j in range(halves):
        kv_ref[:, j * HD : (j + 1) * HD] = fresh[j * count : (j + 1) * count].astype(BF16)
    mean = stats_ref[:rows, :]
    level = stats_ref[rows:, :1]
    spread = [
        jnp.concatenate(
            [
                jnp.broadcast_to(fresh[j * count + b : j * count + b + 1], (heads, HD))
                for b in range(count)
            ],
            axis=0,
        )
        for j in range(halves)
    ]
    own = jnp.sum(q_ref[...] * spread[0], axis=1, keepdims=True) * HD ** (-0.5)
    share = 1.0 / (1.0 + jnp.exp(level - own))
    wide_ref[...] = mean + share * (spread[1] - mean)
    for h in range(heads):
        out_ref[:, h * HD : (h + 1) * HD] = wide_ref[pl.ds(h, count, stride=heads), :].astype(BF16)


def shards(
    hidden, adapter_ids, home_slot, lengths, query, kv_base, cache, adapter_down, adapter_up
):
    per_dev = hidden.shape[0]
    slots, ranks, width = adapter_up.shape
    parts = lax.axis_size("req")
    everyone = per_dev * parts
    block = hidden.shape[1] // parts
    heads = query.shape[1] // HD
    span = ranks * width
    wide = max(block, span)
    center = (parts // 2 + 1) % parts
    order = [(center + p) % parts for p in range(parts)]
    depth = -(-slots // 8) * 8
    core = lax.axis_index("tp").astype(jnp.int32)
    swap = [(0, 1), (1, 0)]
    blocks_shape = jax.ShapeDtypeStruct((parts, per_dev, wide), BF16)
    tall = span // HD * per_dev
    trade_shape = jax.ShapeDtypeStruct((tall + 16, HD), BF16)

    def pin(x):
        return pltpu.with_memory_space_constraint(x, pltpu.HBM)

    def exchange(x):
        return lax.all_to_all(
            x, "req", split_axis=0, concat_axis=0, tiled=True, axis_index_groups=[order]
        )

    ids = adapter_ids.reshape(1, everyone)
    home = home_slot.reshape(1, ADAPTERS)
    like = lambda x: jax.ShapeDtypeStruct(x.shape, x.dtype)
    blocks, near_ids, near_home, near_up = pl.pallas_call(
        start_kernel,
        out_shape=(blocks_shape, like(ids), like(home), like(adapter_up)),
        in_specs=[HBM] * 4,
        out_specs=(VMEM,) * 4,
        scratch_shapes=[pltpu.SemaphoreType.DMA((5,))],
        compiler_params=PARAMS,
    )(
        pin(jnp.swapaxes(hidden.reshape(per_dev, parts, block), 0, 1)),
        pin(ids),
        pin(home),
        pin(adapter_up),
    )
    blocks, near_down, lower = lax.optimization_barrier((blocks, adapter_down, core == 0))
    far_down = lax.ppermute(near_down, "tp", swap)
    blocks = pl.pallas_call(
        functools.partial(pack_kernel, order),
        out_shape=blocks_shape,
        in_specs=[VMEM] + [HBM] * 7,
        out_specs=VMEM,
        scratch_shapes=[
            pltpu.VMEM(ids.shape, ids.dtype),
            pltpu.VMEM(home.shape, home.dtype),
            pltpu.VMEM(adapter_up.shape, BF16),
            pltpu.VMEM((depth, span), F32),
            pltpu.VMEM((slots, ranks, width), F32),
            pltpu.SemaphoreType.DMA((3,)),
        ],
        compiler_params=PARAMS,
    )(
        blocks, pin(ids), pin(home), pin(adapter_up),
        pin(cache), pin(near_down), pin(cache), pin(near_down),
    )
    got = exchange(blocks)
    packed = pl.pallas_call(
        functools.partial(low_kernel, order),
        out_shape=jax.ShapeDtypeStruct((parts, per_dev, span + 128), BF16),
        in_specs=[VMEM] * 6,
        out_specs=VMEM,
        scratch_shapes=[
            pltpu.VMEM((depth, span), F32),
            pltpu.VMEM((slots, ranks, width), F32),
        ],
        compiler_params=PARAMS,
    )(near_ids, near_home, near_up, got, near_down, far_down)

    packed, got, lower = lax.optimization_barrier((packed, got, lower))

    def fold(x):
        return pl.pallas_call(
            functools.partial(fold_kernel, ranks, span),
            out_shape=trade_shape,
            in_specs=[VMEM],
            out_specs=VMEM,
            scratch_shapes=[pltpu.VMEM((tall, HD), F32)],
            compiler_params=PARAMS,
        )(x)

    mine = lax.cond(
        lower,
        lambda packed, got: fold(got[:, :, :span]),
        lambda packed, got: fold(exchange(packed)),
        packed, got,
    )
    mine, lengths, query, cache = lax.optimization_barrier((mine, lengths, query, cache))
    other = lax.ppermute(mine, "tp", swap)
    q_rows, stats = pl.pallas_call(
        attend_kernel,
        out_shape=(
            jax.ShapeDtypeStruct((per_dev * heads, HD), F32),
            jax.ShapeDtypeStruct((2 * per_dev * heads, HD), F32),
        ),
        in_specs=[VMEM] * 3,
        out_specs=(VMEM, VMEM),
        cost_estimate=pl.CostEstimate(flops=0, transcendentals=0, bytes_accessed=1 << 22),
        compiler_params=PARAMS,
    )(lengths.reshape(1, per_dev), query, cache)
    new_kv, attended = pl.pallas_call(
        functools.partial(merge_kernel, ranks),
        out_shape=(
            jax.ShapeDtypeStruct(kv_base.shape, BF16),
            jax.ShapeDtypeStruct(query.shape, BF16),
        ),
        in_specs=[VMEM] * 5,
        out_specs=(VMEM, VMEM),
        scratch_shapes=[pltpu.VMEM((per_dev * heads, HD), F32)],
        compiler_params=PARAMS,
    )(mine, other, q_rows, stats, kv_base)
    return (new_kv, attended)


def solution(mesh):
    placed = (
        P(("group", "req"), None),
        P("group"),
        P(),
        P(("group", "req")),
        P(("group", "req"), "tp"),
        P(("group", "req"), None),
        P(("group", "req"), None, None),
        P("req", "tp"),
        P("req", "tp", None),
    )
    return jax.shard_map(
        shards,
        mesh=mesh,
        in_specs=placed,
        out_specs=(P(("group", "req"), None), P(("group", "req"), "tp")),
        check_vma=False,
    )
```

```python
import functools

import jax
import jax.numpy as jnp
from jax import lax
from jax.experimental import pallas as pl
from jax.experimental.pallas import tpu as pltpu
from jax.sharding import PartitionSpec as P

HD = 128
ADAPTERS = 64
F32 = jnp.float32
BF16 = jnp.bfloat16
VMEM = pl.BlockSpec(memory_space=pltpu.VMEM)
SMEM = pl.BlockSpec(memory_space=pltpu.SMEM)
HBM = pl.BlockSpec(memory_space=pltpu.HBM)
PARAMS = pltpu.CompilerParams(vmem_limit_bytes=8 * 1024 * 1024)


def iota(shape, dim):
    return lax.broadcasted_iota(jnp.int32, shape, dim)


def one_hot_ids(ids):
    shape = (ADAPTERS, ids.shape[1])
    return (iota(shape, 0) == jnp.broadcast_to(ids, shape)).astype(BF16)


def across(a, b):
    return lax.dot_general(a, b, (((0,), (0,)), ((), ())), preferred_element_type=F32)


def start_kernel(
    hidden_ref, ids_hbm, home_hbm, up_hbm, out_ref, ids_ref, home_ref, up_ref, sems
):
    parts, _, block = hidden_ref.shape
    center = (parts // 2 + 1) % parts

    @pl.when(lax.axis_index("tp") == 1)
    def _():
        copies = [
            pltpu.make_async_copy(
                hidden_ref.at[pl.ds(center, parts - center)],
                out_ref.at[pl.ds(0, parts - center), :, pl.ds(0, block)],
                sems.at[0],
            ),
            pltpu.make_async_copy(
                hidden_ref.at[pl.ds(0, center)],
                out_ref.at[pl.ds(parts - center, center), :, pl.ds(0, block)],
                sems.at[1],
            ),
            pltpu.make_async_copy(ids_hbm, ids_ref, sems.at[2]),
            pltpu.make_async_copy(home_hbm, home_ref, sems.at[3]),
            pltpu.make_async_copy(up_hbm, up_ref, sems.at[4]),
        ]
        for copy in copies:
            copy.start()
        for copy in copies:
            copy.wait()


def needed_rows(ids, home, up_ref, flat_ref, wide_ref):
    slots, ranks, width = up_ref.shape
    depth = flat_ref.shape[0]
    if depth > slots:
        flat_ref[...] = jnp.zeros_like(flat_ref)
    wide_ref[...] = up_ref[...].astype(F32)
    for r in range(ranks):
        flat_ref[:slots, r * width : (r + 1) * width] = wide_ref[:, r, :]
    shape = (depth, ADAPTERS)
    base = lax.axis_index("req").astype(jnp.int32) * slots
    here = jnp.broadcast_to(home, shape) - base == iota(shape, 0)
    held = here & (iota(shape, 0) < slots)
    match = jnp.dot(held.astype(BF16), one_hot_ids(ids), preferred_element_type=F32)
    return across(match.astype(BF16), flat_ref[...].astype(BF16)).astype(BF16)


def pack_kernel(
    order, blocks_ref, ids_hbm, home_hbm, up_hbm, cache_hbm, down_hbm, *rest
):
    pack(order, blocks_ref, ids_hbm, home_hbm, up_hbm, *rest[2:])


def pack(
    order, blocks_ref, ids_hbm, home_hbm, up_hbm, out_ref,
    ids_ref, home_ref, up_ref, flat_ref, wide_ref, sems
):
    count = out_ref.shape[1]
    span = flat_ref.shape[1]
    lower = lax.axis_index("tp") == 0

    @pl.when(lower)
    def _():
        pairs = ((ids_hbm, ids_ref), (home_hbm, home_ref), (up_hbm, up_ref))
        copies = [pltpu.make_async_copy(a, b, sems.at[i]) for i, (a, b) in enumerate(pairs)]
        for copy in copies:
            copy.start()
        for copy in copies:
            copy.wait()
        rows = needed_rows(ids_ref[...], home_ref[...], up_ref, flat_ref, wide_ref)
        for p, q in enumerate(order):
            out_ref[p, :, :span] = rows[q * count : (q + 1) * count]

    @pl.when(jnp.logical_not(lower))
    def _():
        out_ref[...] = blocks_ref[...]


def low_kernel(
    order, ids_ref, home_ref, up_ref, got_ref, down_ref, far_ref, out_ref, flat_ref, wide_ref
):
    parts, per_dev, _ = out_ref.shape
    block, columns = down_ref.shape
    ranks = columns // ADAPTERS
    span = flat_ref.shape[1]

    @pl.when(lax.axis_index("tp") == 1)
    def _():
        pieces = [got_ref[p].astype(F32)[:, :block] for p in range(parts)]
        blocks = jnp.concatenate(pieces, axis=0).astype(BF16)
        names = across(one_hot_ids(ids_ref[...]), iota((ADAPTERS, 128), 0).astype(BF16))
        names = names.astype(jnp.int32)
        shift = order[0] * per_dev
        if shift:
            names = jnp.concatenate([names[shift:], names[:shift]], axis=0)
        lane = iota(names.shape, 1)
        spot = names + lane % 2 * ADAPTERS
        rank = lane % (2 * ranks)
        low = jnp.zeros(names.shape, F32)
        for half, ref in enumerate((far_ref, down_ref)):
            for j in range(columns // 128):
                values = jnp.dot(
                    blocks, ref[:, j * 128 : (j + 1) * 128], preferred_element_type=F32
                )
                got = jnp.take_along_axis(values, spot, axis=1)
                low = jnp.where(rank // 2 == j + half * ranks // 2, got, low)
        high = low.astype(BF16).astype(F32)
        low = jnp.where(lane < 2 * ranks, high, low - high).astype(BF16)
        rows = needed_rows(ids_ref[...], home_ref[...], up_ref, flat_ref, wide_ref)
        for p, q in enumerate(order):
            out_ref[p, :, :span] = rows[q * per_dev : (q + 1) * per_dev]
            out_ref[p, :, span:] = low[p * per_dev : (p + 1) * per_dev]


def fold_kernel(ranks, span, got_ref, out_ref, wide_ref):
    total = got_ref[0].astype(F32)
    for p in range(1, got_ref.shape[0]):
        total = total + got_ref[p].astype(F32)
    count = total.shape[0]
    tall = span // HD * count
    for j in range(span // HD):
        wide_ref[j * count : (j + 1) * count, :] = total[:, j * HD : (j + 1) * HD]
    out_ref[:tall, :] = wide_ref[...].astype(BF16)
    if total.shape[1] == span + 128:
        low = total[:, span:]
        low = low + pltpu.roll(low, 128 - 2 * ranks, 1)
        out_ref[tall:, :] = jnp.concatenate([low] * (16 // count), axis=0).astype(BF16)


def early_kernel(
    low_ref, lengths_hbm, query_hbm, cache_hbm, q_ref, stats_ref,
    lengths_ref, query_ref, cache_ref, sems
):
    @pl.when(lax.axis_index("tp") == 0)
    def _():
        early(lengths_hbm, query_hbm, cache_hbm, q_ref, stats_ref,
              lengths_ref, query_ref, cache_ref, sems)


def early(
    lengths_hbm, query_hbm, cache_hbm, q_ref, stats_ref, lengths_ref, query_ref, cache_ref, sems
):
    pairs = ((lengths_hbm, lengths_ref), (query_hbm, query_ref), (cache_hbm, cache_ref))
    copies = [pltpu.make_async_copy(a, b, sems.at[i]) for i, (a, b) in enumerate(pairs)]
    for copy in copies:
        copy.start()
    for copy in copies:
        copy.wait()
    attend(lengths_ref, query_ref, cache_ref, q_ref, stats_ref)


def late_kernel(lengths_ref, query_ref, cache_ref, q_ref, stats_ref):
    @pl.when(lax.axis_index("tp") == 1)
    def _():
        attend(lengths_ref, query_ref, cache_ref, q_ref, stats_ref)


def attend(lengths_ref, query_ref, cache_ref, q_ref, stats_ref):
    count = cache_ref.shape[0]
    heads = query_ref.shape[1] // HD
    scale = HD ** (-0.5)
    query = query_ref[...].astype(F32)
    lengths = lengths_ref[...]
    for h in range(heads):
        q_ref[pl.ds(h, count, stride=heads), :] = query[:, h * HD : (h + 1) * HD]
    for b in range(count):
        part = slice(b * heads, (b + 1) * heads)
        scores = lax.dot_general(
            q_ref[part, :].astype(BF16),
            cache_ref[b, :, :HD],
            (((1,), (1,)), ((), ())),
            preferred_element_type=F32,
        )
        valid = iota(scores.shape, 1) < lengths[:, b : b + 1]
        scores = jnp.where(valid, scores * scale, -jnp.inf)
        top = jnp.max(scores, axis=1, keepdims=True)
        weights = jnp.exp(scores - top)
        total = jnp.sum(weights, axis=1, keepdims=True)
        acc = jnp.dot(weights.astype(BF16), cache_ref[b, :, HD:], preferred_element_type=F32)
        stats_ref[part, :] = acc / total
        after = slice((count + b) * heads, (count + b + 1) * heads)
        stats_ref[after, :] = jnp.broadcast_to(top + jnp.log(total), acc.shape)


def merge_kernel(
    ranks, mine_ref, other_ref, q_ref, stats_ref, early_q_ref, early_ref, base_ref,
    kv_ref, out_ref, wide_ref
):
    count, width = base_ref.shape
    rows = q_ref.shape[0]
    heads = rows // count
    halves = width // HD
    tile = halves * count
    span = ranks * tile
    lower = lax.axis_index("tp") == 0
    base = base_ref[...].astype(F32)
    fresh = jnp.concatenate([base[:, j * HD : (j + 1) * HD] for j in range(halves)], axis=0)
    low = jnp.where(lower, other_ref[span:, :], mine_ref[span:, :]).astype(F32)[:tile]
    for r in range(0, ranks, 16 // tile):
        part = slice(r * tile, r * tile + 16)
        mine = mine_ref[part, :]
        other = other_ref[part, :]
        for half, pair in ((0, jnp.where(lower, mine, other)), (1, jnp.where(lower, other, mine))):
            pair = pair.astype(F32)
            for i in range(16 // tile):
                at = half * ranks + r + i
                fresh = fresh + low[:, at : at + 1] * pair[i * tile : (i + 1) * tile]
    fresh = fresh.astype(BF16).astype(F32)
    for j in range(halves):
        kv_ref[:, j * HD : (j + 1) * HD] = fresh[j * count : (j + 1) * count].astype(BF16)
    stats = jnp.where(lower, early_ref[...], stats_ref[...])
    query = jnp.where(lower, early_q_ref[...], q_ref[...])
    mean = stats[:rows]
    level = stats[rows:, :1]
    spread = [
        jnp.concatenate(
            [
                jnp.broadcast_to(fresh[j * count + b : j * count + b + 1], (heads, HD))
                for b in range(count)
            ],
            axis=0,
        )
        for j in range(halves)
    ]
    own = jnp.sum(query * spread[0], axis=1, keepdims=True) * HD ** (-0.5)
    share = 1.0 / (1.0 + jnp.exp(level - own))
    wide_ref[...] = mean + share * (spread[1] - mean)
    for h in range(heads):
        out_ref[:, h * HD : (h + 1) * HD] = wide_ref[pl.ds(h, count, stride=heads), :].astype(BF16)


def shards(
    hidden, adapter_ids, home_slot, lengths, query, kv_base, cache, adapter_down, adapter_up
):
    per_dev = hidden.shape[0]
    slots, ranks, width = adapter_up.shape
    parts = lax.axis_size("req")
    everyone = per_dev * parts
    block = hidden.shape[1] // parts
    heads = query.shape[1] // HD
    span = ranks * width
    wide = max(block, span)
    center = (parts // 2 + 1) % parts
    order = [(center + p) % parts for p in range(parts)]
    depth = -(-slots // 8) * 8
    core = lax.axis_index("tp").astype(jnp.int32)
    swap = [(0, 1), (1, 0)]
    blocks_shape = jax.ShapeDtypeStruct((parts, per_dev, wide), BF16)
    tall = span // HD * per_dev
    trade_shape = jax.ShapeDtypeStruct((tall + 16, HD), BF16)

    def pin(x):
        return pltpu.with_memory_space_constraint(x, pltpu.HBM)

    def exchange(x):
        return lax.all_to_all(
            x, "req", split_axis=0, concat_axis=0, tiled=True, axis_index_groups=[order]
        )

    ids = adapter_ids.reshape(1, everyone)
    home = home_slot.reshape(1, ADAPTERS)
    like = lambda x: jax.ShapeDtypeStruct(x.shape, x.dtype)
    blocks, near_ids, near_home, near_up = pl.pallas_call(
        start_kernel,
        out_shape=(blocks_shape, like(ids), like(home), like(adapter_up)),
        in_specs=[HBM] * 4,
        out_specs=(VMEM,) * 4,
        scratch_shapes=[pltpu.SemaphoreType.DMA((5,))],
        compiler_params=PARAMS,
    )(
        pin(jnp.swapaxes(hidden.reshape(per_dev, parts, block), 0, 1)),
        pin(ids),
        pin(home),
        pin(adapter_up),
    )
    blocks, near_down, lower = lax.optimization_barrier((blocks, adapter_down, core == 0))
    far_down = lax.ppermute(near_down, "tp", swap)
    blocks = pl.pallas_call(
        functools.partial(pack_kernel, order),
        out_shape=blocks_shape,
        in_specs=[VMEM] + [HBM] * 7,
        out_specs=VMEM,
        scratch_shapes=[
            pltpu.VMEM(ids.shape, ids.dtype),
            pltpu.VMEM(home.shape, home.dtype),
            pltpu.VMEM(adapter_up.shape, BF16),
            pltpu.VMEM((depth, span), F32),
            pltpu.VMEM((slots, ranks, width), F32),
            pltpu.SemaphoreType.DMA((3,)),
        ],
        compiler_params=PARAMS,
    )(
        blocks, pin(ids), pin(home), pin(adapter_up),
        pin(cache), pin(near_down), pin(cache), pin(near_down),
    )
    got = exchange(blocks)
    packed = pl.pallas_call(
        functools.partial(low_kernel, order),
        out_shape=jax.ShapeDtypeStruct((parts, per_dev, span + 128), BF16),
        in_specs=[VMEM] * 6,
        out_specs=VMEM,
        scratch_shapes=[
            pltpu.VMEM((depth, span), F32),
            pltpu.VMEM((slots, ranks, width), F32),
        ],
        compiler_params=PARAMS,
    )(near_ids, near_home, near_up, got, near_down, far_down)

    packed, got, lower = lax.optimization_barrier((packed, got, lower))

    def fold(x):
        return pl.pallas_call(
            functools.partial(fold_kernel, ranks, span),
            out_shape=trade_shape,
            in_specs=[VMEM],
            out_specs=VMEM,
            scratch_shapes=[pltpu.VMEM((tall, HD), F32)],
            compiler_params=PARAMS,
        )(x)

    heads_shape = jax.ShapeDtypeStruct((per_dev * heads, HD), F32)
    stats_shape = jax.ShapeDtypeStruct((2 * per_dev * heads, HD), F32)

    early_q, early_stats = pl.pallas_call(
        early_kernel,
        out_shape=(heads_shape, stats_shape),
        in_specs=[VMEM] + [HBM] * 3,
        out_specs=(VMEM, VMEM),
        scratch_shapes=[
            pltpu.VMEM((1, per_dev), lengths.dtype),
            pltpu.VMEM(query.shape, BF16),
            pltpu.VMEM(cache.shape, BF16),
            pltpu.SemaphoreType.DMA((3,)),
        ],
        compiler_params=PARAMS,
    )(packed, pin(lengths.reshape(1, per_dev)), pin(query), pin(cache))
    packed, got, early_q = lax.optimization_barrier((packed, got, early_q))
    mine = lax.cond(
        lower,
        lambda packed, got: fold(got[:, :, :span]),
        lambda packed, got: fold(exchange(packed)),
        packed, got,
    )
    mine, lengths, query, cache = lax.optimization_barrier((mine, lengths, query, cache))
    other = lax.ppermute(mine, "tp", swap)
    q_rows, stats = pl.pallas_call(
        late_kernel,
        out_shape=(heads_shape, stats_shape),
        in_specs=[VMEM] * 3,
        out_specs=(VMEM, VMEM),
        cost_estimate=pl.CostEstimate(flops=0, transcendentals=0, bytes_accessed=1 << 22),
        compiler_params=PARAMS,
    )(lengths.reshape(1, per_dev), query, cache)
    new_kv, attended = pl.pallas_call(
        functools.partial(merge_kernel, ranks),
        out_shape=(
            jax.ShapeDtypeStruct(kv_base.shape, BF16),
            jax.ShapeDtypeStruct(query.shape, BF16),
        ),
        in_specs=[VMEM] * 7,
        out_specs=(VMEM, VMEM),
        scratch_shapes=[pltpu.VMEM((per_dev * heads, HD), F32)],
        compiler_params=PARAMS,
    )(mine, other, q_rows, stats, early_q, early_stats, kv_base)
    return (new_kv, attended)


def solution(mesh):
    placed = (
        P(("group", "req"), None),
        P("group"),
        P(),
        P(("group", "req")),
        P(("group", "req"), "tp"),
        P(("group", "req"), None),
        P(("group", "req"), None, None),
        P("req", "tp"),
        P("req", "tp", None),
    )
    return jax.shard_map(
        shards,
        mesh=mesh,
        in_specs=placed,
        out_specs=(P(("group", "req"), None), P(("group", "req"), "tp")),
        check_vma=False,
    )
```

```python
import functools

import jax
import jax.numpy as jnp
from jax import lax
from jax.experimental import pallas as pl
from jax.experimental.pallas import tpu as pltpu
from jax.sharding import PartitionSpec as P

HD = 128
ADAPTERS = 64
F32 = jnp.float32
BF16 = jnp.bfloat16
VMEM = pl.BlockSpec(memory_space=pltpu.VMEM)
SMEM = pl.BlockSpec(memory_space=pltpu.SMEM)
HBM = pl.BlockSpec(memory_space=pltpu.HBM)
PARAMS = pltpu.CompilerParams(vmem_limit_bytes=8 * 1024 * 1024)


def iota(shape, dim):
    return lax.broadcasted_iota(jnp.int32, shape, dim)


def one_hot_ids(ids):
    shape = (ADAPTERS, ids.shape[1])
    return (iota(shape, 0) == jnp.broadcast_to(ids, shape)).astype(BF16)


def across(a, b):
    return lax.dot_general(a, b, (((0,), (0,)), ((), ())), preferred_element_type=F32)


def runs(order):
    found = []
    for p, q in enumerate(order):
        if p and q == order[p - 1] + 1:
            found[-1] = (found[-1][0], found[-1][1] + 1)
        else:
            found.append((p, 1))
    return found


def start_kernel(
    order, hidden_ref, ids_hbm, home_hbm, up_hbm, out_ref, ids_ref, home_ref, up_ref, sems
):
    parts, _, block = hidden_ref.shape

    @pl.when(lax.axis_index("tp") == 1)
    def _():
        copies = [
            *(
                pltpu.make_async_copy(
                    hidden_ref.at[pl.ds(order[at], count)],
                    out_ref.at[pl.ds(at, count), :, pl.ds(0, block)],
                    sems.at[5 + i],
                )
                for i, (at, count) in enumerate(runs(order))
            ),
            pltpu.make_async_copy(ids_hbm, ids_ref, sems.at[2]),
            pltpu.make_async_copy(home_hbm, home_ref, sems.at[3]),
            pltpu.make_async_copy(up_hbm, up_ref, sems.at[4]),
        ]
        for copy in copies:
            copy.start()
        for copy in copies:
            copy.wait()


def needed_rows(ids, home, up_ref, flat_ref, wide_ref):
    slots, ranks, width = up_ref.shape
    depth = flat_ref.shape[0]
    if depth > slots:
        flat_ref[...] = jnp.zeros_like(flat_ref)
    wide_ref[...] = up_ref[...].astype(F32)
    for r in range(ranks):
        flat_ref[:slots, r * width : (r + 1) * width] = wide_ref[:, r, :]
    shape = (depth, ADAPTERS)
    base = lax.axis_index("req").astype(jnp.int32) * slots
    here = jnp.broadcast_to(home, shape) - base == iota(shape, 0)
    held = here & (iota(shape, 0) < slots)
    match = jnp.dot(held.astype(BF16), one_hot_ids(ids), preferred_element_type=F32)
    return across(match.astype(BF16), flat_ref[...].astype(BF16)).astype(BF16)


def pack_kernel(
    order, blocks_ref, ids_hbm, home_hbm, up_hbm, cache_hbm, down_hbm, *rest
):
    pack(order, blocks_ref, ids_hbm, home_hbm, up_hbm, *rest[2:])


def pack(
    order, blocks_ref, ids_hbm, home_hbm, up_hbm, out_ref,
    ids_ref, home_ref, up_ref, flat_ref, wide_ref, sems
):
    count = out_ref.shape[1]
    span = flat_ref.shape[1]
    lower = lax.axis_index("tp") == 0

    @pl.when(lower)
    def _():
        pairs = ((ids_hbm, ids_ref), (home_hbm, home_ref), (up_hbm, up_ref))
        copies = [pltpu.make_async_copy(a, b, sems.at[i]) for i, (a, b) in enumerate(pairs)]
        for copy in copies:
            copy.start()
        for copy in copies:
            copy.wait()
        rows = needed_rows(ids_ref[...], home_ref[...], up_ref, flat_ref, wide_ref)
        for p, q in enumerate(order):
            out_ref[p, :, :span] = rows[q * count : (q + 1) * count]

    @pl.when(jnp.logical_not(lower))
    def _():
        out_ref[...] = blocks_ref[...]


def low_kernel(
    order, ids_ref, home_ref, up_ref, got_ref, down_ref, far_ref, out_ref, flat_ref, wide_ref
):
    parts, per_dev, _ = out_ref.shape
    block, columns = down_ref.shape
    ranks = columns // ADAPTERS
    span = flat_ref.shape[1]

    @pl.when(lax.axis_index("tp") == 1)
    def _():
        pieces = [got_ref[p].astype(F32)[:, :block] for p in range(parts)]
        blocks = jnp.concatenate(pieces, axis=0).astype(BF16)
        names = across(one_hot_ids(ids_ref[...]), iota((ADAPTERS, 128), 0).astype(BF16))
        names = names.astype(jnp.int32)
        names = jnp.concatenate(
            [
                names[order[at] * per_dev : (order[at] + count) * per_dev]
                for at, count in runs(order)
            ],
            axis=0,
        )
        lane = iota(names.shape, 1)
        spot = names + lane % 2 * ADAPTERS
        rank = lane % (2 * ranks)
        low = jnp.zeros(names.shape, F32)
        for half, ref in enumerate((far_ref, down_ref)):
            for j in range(columns // 128):
                values = jnp.dot(
                    blocks, ref[:, j * 128 : (j + 1) * 128], preferred_element_type=F32
                )
                got = jnp.take_along_axis(values, spot, axis=1)
                low = jnp.where(rank // 2 == j + half * ranks // 2, got, low)
        high = low.astype(BF16).astype(F32)
        low = jnp.where(lane < 2 * ranks, high, low - high).astype(BF16)
        rows = needed_rows(ids_ref[...], home_ref[...], up_ref, flat_ref, wide_ref)
        for p, q in enumerate(order):
            out_ref[p, :, :span] = rows[q * per_dev : (q + 1) * per_dev]
            out_ref[p, :, span:] = low[p * per_dev : (p + 1) * per_dev]


def fold_kernel(ranks, span, got_ref, out_ref, wide_ref):
    total = got_ref[0].astype(F32)
    for p in range(1, got_ref.shape[0]):
        total = total + got_ref[p].astype(F32)
    count = total.shape[0]
    tall = span // HD * count
    for j in range(span // HD):
        wide_ref[j * count : (j + 1) * count, :] = total[:, j * HD : (j + 1) * HD]
    out_ref[:tall, :] = wide_ref[...].astype(BF16)
    if total.shape[1] == span + 128:
        low = total[:, span:]
        low = low + pltpu.roll(low, 128 - 2 * ranks, 1)
        out_ref[tall:, :] = jnp.concatenate([low] * (16 // count), axis=0).astype(BF16)


def early_kernel(
    low_ref, lengths_hbm, query_hbm, cache_hbm, q_ref, stats_ref,
    lengths_ref, query_ref, cache_ref, sems
):
    @pl.when(lax.axis_index("tp") == 0)
    def _():
        early(lengths_hbm, query_hbm, cache_hbm, q_ref, stats_ref,
              lengths_ref, query_ref, cache_ref, sems)


def early(
    lengths_hbm, query_hbm, cache_hbm, q_ref, stats_ref, lengths_ref, query_ref, cache_ref, sems
):
    pairs = ((lengths_hbm, lengths_ref), (query_hbm, query_ref), (cache_hbm, cache_ref))
    copies = [pltpu.make_async_copy(a, b, sems.at[i]) for i, (a, b) in enumerate(pairs)]
    for copy in copies:
        copy.start()
    for copy in copies:
        copy.wait()
    attend(lengths_ref, query_ref, cache_ref, q_ref, stats_ref)


def late_kernel(lengths_ref, query_ref, cache_ref, q_ref, stats_ref):
    @pl.when(lax.axis_index("tp") == 1)
    def _():
        attend(lengths_ref, query_ref, cache_ref, q_ref, stats_ref)


def attend(lengths_ref, query_ref, cache_ref, q_ref, stats_ref):
    count = cache_ref.shape[0]
    heads = query_ref.shape[1] // HD
    scale = HD ** (-0.5)
    query = query_ref[...].astype(F32)
    lengths = lengths_ref[...]
    for h in range(heads):
        q_ref[pl.ds(h, count, stride=heads), :] = query[:, h * HD : (h + 1) * HD]
    for b in range(count):
        part = slice(b * heads, (b + 1) * heads)
        scores = lax.dot_general(
            q_ref[part, :].astype(BF16),
            cache_ref[b, :, :HD],
            (((1,), (1,)), ((), ())),
            preferred_element_type=F32,
        )
        valid = iota(scores.shape, 1) < lengths[:, b : b + 1]
        scores = jnp.where(valid, scores * scale, -jnp.inf)
        top = jnp.max(scores, axis=1, keepdims=True)
        weights = jnp.exp(scores - top)
        total = jnp.sum(weights, axis=1, keepdims=True)
        acc = jnp.dot(weights.astype(BF16), cache_ref[b, :, HD:], preferred_element_type=F32)
        stats_ref[part, :] = acc / total
        after = slice((count + b) * heads, (count + b + 1) * heads)
        stats_ref[after, :] = jnp.broadcast_to(top + jnp.log(total), acc.shape)


def merge_kernel(
    ranks, mine_ref, other_ref, q_ref, stats_ref, early_q_ref, early_ref, base_ref,
    kv_ref, out_ref, wide_ref
):
    count, width = base_ref.shape
    rows = q_ref.shape[0]
    heads = rows // count
    halves = width // HD
    tile = halves * count
    span = ranks * tile
    lower = lax.axis_index("tp") == 0
    base = base_ref[...].astype(F32)
    fresh = jnp.concatenate([base[:, j * HD : (j + 1) * HD] for j in range(halves)], axis=0)
    low = jnp.where(lower, other_ref[span:, :], mine_ref[span:, :]).astype(F32)[:tile]
    for r in range(0, ranks, 16 // tile):
        part = slice(r * tile, r * tile + 16)
        mine = mine_ref[part, :]
        other = other_ref[part, :]
        for half, pair in ((0, jnp.where(lower, mine, other)), (1, jnp.where(lower, other, mine))):
            pair = pair.astype(F32)
            for i in range(16 // tile):
                at = half * ranks + r + i
                fresh = fresh + low[:, at : at + 1] * pair[i * tile : (i + 1) * tile]
    fresh = fresh.astype(BF16).astype(F32)
    for j in range(halves):
        kv_ref[:, j * HD : (j + 1) * HD] = fresh[j * count : (j + 1) * count].astype(BF16)
    stats = jnp.where(lower, early_ref[...], stats_ref[...])
    query = jnp.where(lower, early_q_ref[...], q_ref[...])
    mean = stats[:rows]
    level = stats[rows:, :1]
    spread = [
        jnp.concatenate(
            [
                jnp.broadcast_to(fresh[j * count + b : j * count + b + 1], (heads, HD))
                for b in range(count)
            ],
            axis=0,
        )
        for j in range(halves)
    ]
    own = jnp.sum(query * spread[0], axis=1, keepdims=True) * HD ** (-0.5)
    share = 1.0 / (1.0 + jnp.exp(level - own))
    wide_ref[...] = mean + share * (spread[1] - mean)
    for h in range(heads):
        out_ref[:, h * HD : (h + 1) * HD] = wide_ref[pl.ds(h, count, stride=heads), :].astype(BF16)


def shards(
    hidden, adapter_ids, home_slot, lengths, query, kv_base, cache, adapter_down, adapter_up
):
    per_dev = hidden.shape[0]
    slots, ranks, width = adapter_up.shape
    parts = lax.axis_size("req")
    everyone = per_dev * parts
    block = hidden.shape[1] // parts
    heads = query.shape[1] // HD
    span = ranks * width
    wide = max(block, span)
    center = (parts // 2 + 1) % parts
    order = [center, 0, *range(center + 1, parts), *range(1, center)] if center else [*range(parts)]
    depth = -(-slots // 8) * 8
    core = lax.axis_index("tp").astype(jnp.int32)
    swap = [(0, 1), (1, 0)]
    blocks_shape = jax.ShapeDtypeStruct((parts, per_dev, wide), BF16)
    tall = span // HD * per_dev
    trade_shape = jax.ShapeDtypeStruct((tall + 16, HD), BF16)

    def pin(x):
        return pltpu.with_memory_space_constraint(x, pltpu.HBM)

    def exchange(x):
        return lax.all_to_all(
            x, "req", split_axis=0, concat_axis=0, tiled=True, axis_index_groups=[order]
        )

    ids = adapter_ids.reshape(1, everyone)
    home = home_slot.reshape(1, ADAPTERS)
    like = lambda x: jax.ShapeDtypeStruct(x.shape, x.dtype)
    blocks, near_ids, near_home, near_up = pl.pallas_call(
        functools.partial(start_kernel, order),
        out_shape=(blocks_shape, like(ids), like(home), like(adapter_up)),
        in_specs=[HBM] * 4,
        out_specs=(VMEM,) * 4,
        scratch_shapes=[pltpu.SemaphoreType.DMA((5 + len(runs(order)),))],
        compiler_params=PARAMS,
    )(
        pin(jnp.swapaxes(hidden.reshape(per_dev, parts, block), 0, 1)),
        pin(ids),
        pin(home),
        pin(adapter_up),
    )
    blocks, near_down, lower = lax.optimization_barrier((blocks, adapter_down, core == 0))
    far_down = lax.ppermute(near_down, "tp", swap)
    blocks = pl.pallas_call(
        functools.partial(pack_kernel, order),
        out_shape=blocks_shape,
        in_specs=[VMEM] + [HBM] * 7,
        out_specs=VMEM,
        scratch_shapes=[
            pltpu.VMEM(ids.shape, ids.dtype),
            pltpu.VMEM(home.shape, home.dtype),
            pltpu.VMEM(adapter_up.shape, BF16),
            pltpu.VMEM((depth, span), F32),
            pltpu.VMEM((slots, ranks, width), F32),
            pltpu.SemaphoreType.DMA((3,)),
        ],
        compiler_params=PARAMS,
    )(
        blocks, pin(ids), pin(home), pin(adapter_up),
        pin(cache), pin(near_down), pin(cache), pin(near_down),
    )
    got = exchange(blocks)
    packed = pl.pallas_call(
        functools.partial(low_kernel, order),
        out_shape=jax.ShapeDtypeStruct((parts, per_dev, span + 128), BF16),
        in_specs=[VMEM] * 6,
        out_specs=VMEM,
        scratch_shapes=[
            pltpu.VMEM((depth, span), F32),
            pltpu.VMEM((slots, ranks, width), F32),
        ],
        compiler_params=PARAMS,
    )(near_ids, near_home, near_up, got, near_down, far_down)

    packed, got, lower = lax.optimization_barrier((packed, got, lower))

    def fold(x):
        return pl.pallas_call(
            functools.partial(fold_kernel, ranks, span),
            out_shape=trade_shape,
            in_specs=[VMEM],
            out_specs=VMEM,
            scratch_shapes=[pltpu.VMEM((tall, HD), F32)],
            compiler_params=PARAMS,
        )(x)

    heads_shape = jax.ShapeDtypeStruct((per_dev * heads, HD), F32)
    stats_shape = jax.ShapeDtypeStruct((2 * per_dev * heads, HD), F32)

    early_q, early_stats = pl.pallas_call(
        early_kernel,
        out_shape=(heads_shape, stats_shape),
        in_specs=[VMEM] + [HBM] * 3,
        out_specs=(VMEM, VMEM),
        scratch_shapes=[
            pltpu.VMEM((1, per_dev), lengths.dtype),
            pltpu.VMEM(query.shape, BF16),
            pltpu.VMEM(cache.shape, BF16),
            pltpu.SemaphoreType.DMA((3,)),
        ],
        compiler_params=PARAMS,
    )(packed, pin(lengths.reshape(1, per_dev)), pin(query), pin(cache))
    packed, got, early_q = lax.optimization_barrier((packed, got, early_q))
    mine = lax.cond(
        lower,
        lambda packed, got: fold(got[:, :, :span]),
        lambda packed, got: fold(exchange(packed)),
        packed, got,
    )
    mine, lengths, query, cache = lax.optimization_barrier((mine, lengths, query, cache))
    other = lax.ppermute(mine, "tp", swap)
    q_rows, stats = pl.pallas_call(
        late_kernel,
        out_shape=(heads_shape, stats_shape),
        in_specs=[VMEM] * 3,
        out_specs=(VMEM, VMEM),
        cost_estimate=pl.CostEstimate(flops=0, transcendentals=0, bytes_accessed=1 << 22),
        compiler_params=PARAMS,
    )(lengths.reshape(1, per_dev), query, cache)
    new_kv, attended = pl.pallas_call(
        functools.partial(merge_kernel, ranks),
        out_shape=(
            jax.ShapeDtypeStruct(kv_base.shape, BF16),
            jax.ShapeDtypeStruct(query.shape, BF16),
        ),
        in_specs=[VMEM] * 7,
        out_specs=(VMEM, VMEM),
        scratch_shapes=[pltpu.VMEM((per_dev * heads, HD), F32)],
        compiler_params=PARAMS,
    )(mine, other, q_rows, stats, early_q, early_stats, kv_base)
    return (new_kv, attended)


def solution(mesh):
    placed = (
        P(("group", "req"), None),
        P("group"),
        P(),
        P(("group", "req")),
        P(("group", "req"), "tp"),
        P(("group", "req"), None),
        P(("group", "req"), None, None),
        P("req", "tp"),
        P("req", "tp", None),
    )
    return jax.shard_map(
        shards,
        mesh=mesh,
        in_specs=placed,
        out_specs=(P(("group", "req"), None), P(("group", "req"), "tp")),
        check_vma=False,
    )
```

```python
import functools

import jax
import jax.numpy as jnp
from jax import lax
from jax.experimental import pallas as pl
from jax.experimental.pallas import tpu as pltpu
from jax.sharding import PartitionSpec as P

HD = 128
ADAPTERS = 64
F32 = jnp.float32
BF16 = jnp.bfloat16
VMEM = pl.BlockSpec(memory_space=pltpu.VMEM)
SMEM = pl.BlockSpec(memory_space=pltpu.SMEM)
HBM = pl.BlockSpec(memory_space=pltpu.HBM)
PARAMS = pltpu.CompilerParams(vmem_limit_bytes=8 * 1024 * 1024)


def iota(shape, dim):
    return lax.broadcasted_iota(jnp.int32, shape, dim)


def one_hot_ids(ids):
    shape = (ADAPTERS, ids.shape[1])
    return (iota(shape, 0) == jnp.broadcast_to(ids, shape)).astype(BF16)


def across(a, b):
    return lax.dot_general(a, b, (((0,), (0,)), ((), ())), preferred_element_type=F32)


def runs(order):
    found = []
    for p, q in enumerate(order):
        if p and q == order[p - 1] + 1:
            found[-1] = (found[-1][0], found[-1][1] + 1)
        else:
            found.append((p, 1))
    return found


def start_kernel(
    order, hidden_ref, ids_hbm, home_hbm, up_hbm, out_ref, ids_ref, home_ref, up_ref, sems
):
    parts, _, block = hidden_ref.shape

    @pl.when(lax.axis_index("tp") == 1)
    def _():
        copies = [
            *(
                pltpu.make_async_copy(
                    hidden_ref.at[pl.ds(order[at], count)],
                    out_ref.at[pl.ds(at, count), :, pl.ds(0, block)],
                    sems.at[5 + i],
                )
                for i, (at, count) in enumerate(runs(order))
            ),
            pltpu.make_async_copy(ids_hbm, ids_ref, sems.at[2]),
            pltpu.make_async_copy(home_hbm, home_ref, sems.at[3]),
            pltpu.make_async_copy(up_hbm, up_ref, sems.at[4]),
        ]
        for copy in copies:
            copy.start()
        for copy in copies:
            copy.wait()


def needed_rows(ids, home, up_ref, flat_ref, wide_ref):
    slots, ranks, width = up_ref.shape
    depth = flat_ref.shape[0]
    if depth > slots:
        flat_ref[...] = jnp.zeros_like(flat_ref)
    wide_ref[...] = up_ref[...].astype(F32)
    for r in range(ranks):
        flat_ref[:slots, r * width : (r + 1) * width] = wide_ref[:, r, :]
    shape = (depth, ADAPTERS)
    base = lax.axis_index("req").astype(jnp.int32) * slots
    here = jnp.broadcast_to(home, shape) - base == iota(shape, 0)
    held = here & (iota(shape, 0) < slots)
    match = jnp.dot(held.astype(BF16), one_hot_ids(ids), preferred_element_type=F32)
    return across(match.astype(BF16), flat_ref[...].astype(BF16)).astype(BF16)


def pack_kernel(
    order, blocks_ref, ids_hbm, home_hbm, up_hbm, cache_hbm, down_hbm, *rest
):
    pack(order, blocks_ref, ids_hbm, home_hbm, up_hbm, *rest[2:])


def pack(
    order, blocks_ref, ids_hbm, home_hbm, up_hbm, out_ref,
    ids_ref, home_ref, up_ref, flat_ref, wide_ref, sems
):
    count = out_ref.shape[1]
    span = flat_ref.shape[1]
    lower = lax.axis_index("tp") == 0

    @pl.when(lower)
    def _():
        pairs = ((ids_hbm, ids_ref), (home_hbm, home_ref), (up_hbm, up_ref))
        copies = [pltpu.make_async_copy(a, b, sems.at[i]) for i, (a, b) in enumerate(pairs)]
        for copy in copies:
            copy.start()
        for copy in copies:
            copy.wait()
        rows = needed_rows(ids_ref[...], home_ref[...], up_ref, flat_ref, wide_ref)
        for p, q in enumerate(order):
            out_ref[p, :, :span] = rows[q * count : (q + 1) * count]


def low_kernel(
    order, ids_ref, home_ref, up_ref, got_ref, down_ref, far_ref, out_ref, flat_ref, wide_ref
):
    parts, per_dev, _ = out_ref.shape
    block, columns = down_ref.shape
    ranks = columns // ADAPTERS
    span = flat_ref.shape[1]

    @pl.when(lax.axis_index("tp") == 1)
    def _():
        pieces = [got_ref[p].astype(F32)[:, :block] for p in range(parts)]
        blocks = jnp.concatenate(pieces, axis=0).astype(BF16)
        names = across(one_hot_ids(ids_ref[...]), iota((ADAPTERS, 128), 0).astype(BF16))
        names = names.astype(jnp.int32)
        names = jnp.concatenate(
            [
                names[order[at] * per_dev : (order[at] + count) * per_dev]
                for at, count in runs(order)
            ],
            axis=0,
        )
        lane = iota(names.shape, 1)
        spot = names + lane % 2 * ADAPTERS
        rank = lane % (2 * ranks)
        low = jnp.zeros(names.shape, F32)
        for half, ref in enumerate((far_ref, down_ref)):
            for j in range(columns // 128):
                values = jnp.dot(
                    blocks, ref[:, j * 128 : (j + 1) * 128], preferred_element_type=F32
                )
                got = jnp.take_along_axis(values, spot, axis=1)
                low = jnp.where(rank // 2 == j + half * ranks // 2, got, low)
        high = low.astype(BF16).astype(F32)
        low = jnp.where(lane < 2 * ranks, high, low - high).astype(BF16)
        rows = needed_rows(ids_ref[...], home_ref[...], up_ref, flat_ref, wide_ref)
        for p, q in enumerate(order):
            out_ref[p, :, :span] = rows[q * per_dev : (q + 1) * per_dev]
            out_ref[p, :, span:] = low[p * per_dev : (p + 1) * per_dev]


def fold_kernel(ranks, span, got_ref, out_ref, wide_ref):
    total = got_ref[0].astype(F32)
    for p in range(1, got_ref.shape[0]):
        total = total + got_ref[p].astype(F32)
    count = total.shape[0]
    tall = span // HD * count
    for j in range(span // HD):
        wide_ref[j * count : (j + 1) * count, :] = total[:, j * HD : (j + 1) * HD]
    out_ref[:tall, :] = wide_ref[...].astype(BF16)
    if total.shape[1] == span + 128:
        low = total[:, span:]
        low = low + pltpu.roll(low, 128 - 2 * ranks, 1)
        out_ref[tall:, :] = jnp.concatenate([low] * (16 // count), axis=0).astype(BF16)


def early_kernel(
    low_ref, lengths_hbm, query_hbm, cache_hbm, q_ref, stats_ref,
    lengths_ref, query_ref, cache_ref, sems
):
    @pl.when(lax.axis_index("tp") == 0)
    def _():
        early(lengths_hbm, query_hbm, cache_hbm, q_ref, stats_ref,
              lengths_ref, query_ref, cache_ref, sems)


def early(
    lengths_hbm, query_hbm, cache_hbm, q_ref, stats_ref, lengths_ref, query_ref, cache_ref, sems
):
    pairs = ((lengths_hbm, lengths_ref), (query_hbm, query_ref), (cache_hbm, cache_ref))
    copies = [pltpu.make_async_copy(a, b, sems.at[i]) for i, (a, b) in enumerate(pairs)]
    for copy in copies:
        copy.start()
    for copy in copies:
        copy.wait()
    attend(lengths_ref, query_ref, cache_ref, q_ref, stats_ref)


def late_kernel(lengths_ref, query_ref, cache_ref, q_ref, stats_ref):
    @pl.when(lax.axis_index("tp") == 1)
    def _():
        attend(lengths_ref, query_ref, cache_ref, q_ref, stats_ref)


def attend(lengths_ref, query_ref, cache_ref, q_ref, stats_ref):
    count = cache_ref.shape[0]
    heads = query_ref.shape[1] // HD
    scale = HD ** (-0.5)
    query = query_ref[...].astype(F32)
    lengths = lengths_ref[...]
    for h in range(heads):
        q_ref[pl.ds(h, count, stride=heads), :] = query[:, h * HD : (h + 1) * HD]
    for b in range(count):
        part = slice(b * heads, (b + 1) * heads)
        scores = lax.dot_general(
            q_ref[part, :].astype(BF16),
            cache_ref[b, :, :HD],
            (((1,), (1,)), ((), ())),
            preferred_element_type=F32,
        )
        valid = iota(scores.shape, 1) < lengths[:, b : b + 1]
        scores = jnp.where(valid, scores * scale, -jnp.inf)
        top = jnp.max(scores, axis=1, keepdims=True)
        weights = jnp.exp(scores - top)
        total = jnp.sum(weights, axis=1, keepdims=True)
        acc = jnp.dot(weights.astype(BF16), cache_ref[b, :, HD:], preferred_element_type=F32)
        stats_ref[part, :] = acc / total
        after = slice((count + b) * heads, (count + b + 1) * heads)
        stats_ref[after, :] = jnp.broadcast_to(top + jnp.log(total), acc.shape)


def merge_kernel(
    ranks, mine_ref, other_ref, q_ref, stats_ref, early_q_ref, early_ref, base_ref,
    kv_ref, out_ref, wide_ref
):
    count, width = base_ref.shape
    rows = q_ref.shape[0]
    heads = rows // count
    halves = width // HD
    tile = halves * count
    span = ranks * tile
    lower = lax.axis_index("tp") == 0
    base = base_ref[...].astype(F32)
    fresh = jnp.concatenate([base[:, j * HD : (j + 1) * HD] for j in range(halves)], axis=0)
    low = jnp.where(lower, other_ref[span:, :], mine_ref[span:, :]).astype(F32)[:tile]
    for r in range(0, ranks, 16 // tile):
        part = slice(r * tile, r * tile + 16)
        mine = mine_ref[part, :]
        other = other_ref[part, :]
        for half, pair in ((0, jnp.where(lower, mine, other)), (1, jnp.where(lower, other, mine))):
            pair = pair.astype(F32)
            for i in range(16 // tile):
                at = half * ranks + r + i
                fresh = fresh + low[:, at : at + 1] * pair[i * tile : (i + 1) * tile]
    fresh = fresh.astype(BF16).astype(F32)
    for j in range(halves):
        kv_ref[:, j * HD : (j + 1) * HD] = fresh[j * count : (j + 1) * count].astype(BF16)
    stats = jnp.where(lower, early_ref[...], stats_ref[...])
    query = jnp.where(lower, early_q_ref[...], q_ref[...])
    mean = stats[:rows]
    level = stats[rows:, :1]
    spread = [
        jnp.concatenate(
            [
                jnp.broadcast_to(fresh[j * count + b : j * count + b + 1], (heads, HD))
                for b in range(count)
            ],
            axis=0,
        )
        for j in range(halves)
    ]
    own = jnp.sum(query * spread[0], axis=1, keepdims=True) * HD ** (-0.5)
    share = 1.0 / (1.0 + jnp.exp(level - own))
    wide_ref[...] = mean + share * (spread[1] - mean)
    for h in range(heads):
        out_ref[:, h * HD : (h + 1) * HD] = wide_ref[pl.ds(h, count, stride=heads), :].astype(BF16)


def shards(
    hidden, adapter_ids, home_slot, lengths, query, kv_base, cache, adapter_down, adapter_up
):
    per_dev = hidden.shape[0]
    slots, ranks, width = adapter_up.shape
    parts = lax.axis_size("req")
    everyone = per_dev * parts
    block = hidden.shape[1] // parts
    heads = query.shape[1] // HD
    span = ranks * width
    wide = max(block, span)
    center = (parts // 2 + 1) % parts
    order = [center, 0, *range(center + 1, parts), *range(1, center)] if center else [*range(parts)]
    depth = -(-slots // 8) * 8
    core = lax.axis_index("tp").astype(jnp.int32)
    swap = [(0, 1), (1, 0)]
    blocks_shape = jax.ShapeDtypeStruct((parts, per_dev, wide), BF16)
    tall = span // HD * per_dev
    trade_shape = jax.ShapeDtypeStruct((tall + 16, HD), BF16)

    def pin(x):
        return pltpu.with_memory_space_constraint(x, pltpu.HBM)

    def exchange(x):
        return lax.all_to_all(
            x, "req", split_axis=0, concat_axis=0, tiled=True, axis_index_groups=[order]
        )

    ids = adapter_ids.reshape(1, everyone)
    home = home_slot.reshape(1, ADAPTERS)
    like = lambda x: jax.ShapeDtypeStruct(x.shape, x.dtype)
    blocks, near_ids, near_home, near_up = pl.pallas_call(
        functools.partial(start_kernel, order),
        out_shape=(blocks_shape, like(ids), like(home), like(adapter_up)),
        in_specs=[HBM] * 4,
        out_specs=(VMEM,) * 4,
        scratch_shapes=[pltpu.SemaphoreType.DMA((5 + len(runs(order)),))],
        compiler_params=PARAMS,
    )(
        pin(jnp.swapaxes(hidden.reshape(per_dev, parts, block), 0, 1)),
        pin(ids),
        pin(home),
        pin(adapter_up),
    )
    blocks, near_down, lower = lax.optimization_barrier((blocks, adapter_down, core == 0))
    far_down = lax.ppermute(near_down, "tp", swap)
    blocks = pl.pallas_call(
        functools.partial(pack_kernel, order),
        out_shape=blocks_shape,
        in_specs=[VMEM] + [HBM] * 7,
        out_specs=VMEM,
        scratch_shapes=[
            pltpu.VMEM(ids.shape, ids.dtype),
            pltpu.VMEM(home.shape, home.dtype),
            pltpu.VMEM(adapter_up.shape, BF16),
            pltpu.VMEM((depth, span), F32),
            pltpu.VMEM((slots, ranks, width), F32),
            pltpu.SemaphoreType.DMA((3,)),
        ],
        input_output_aliases={0: 0},
        compiler_params=PARAMS,
    )(
        blocks, pin(ids), pin(home), pin(adapter_up),
        pin(cache), pin(near_down), pin(cache), pin(near_down),
    )
    got = exchange(blocks)
    packed = pl.pallas_call(
        functools.partial(low_kernel, order),
        out_shape=jax.ShapeDtypeStruct((parts, per_dev, span + 128), BF16),
        in_specs=[VMEM] * 6,
        out_specs=VMEM,
        scratch_shapes=[
            pltpu.VMEM((depth, span), F32),
            pltpu.VMEM((slots, ranks, width), F32),
        ],
        compiler_params=PARAMS,
    )(near_ids, near_home, near_up, got, near_down, far_down)

    packed, got, lower = lax.optimization_barrier((packed, got, lower))

    def fold(x):
        return pl.pallas_call(
            functools.partial(fold_kernel, ranks, span),
            out_shape=trade_shape,
            in_specs=[VMEM],
            out_specs=VMEM,
            scratch_shapes=[pltpu.VMEM((tall, HD), F32)],
            compiler_params=PARAMS,
        )(x)

    heads_shape = jax.ShapeDtypeStruct((per_dev * heads, HD), F32)
    stats_shape = jax.ShapeDtypeStruct((2 * per_dev * heads, HD), F32)

    early_q, early_stats = pl.pallas_call(
        early_kernel,
        out_shape=(heads_shape, stats_shape),
        in_specs=[VMEM] + [HBM] * 3,
        out_specs=(VMEM, VMEM),
        scratch_shapes=[
            pltpu.VMEM((1, per_dev), lengths.dtype),
            pltpu.VMEM(query.shape, BF16),
            pltpu.VMEM(cache.shape, BF16),
            pltpu.SemaphoreType.DMA((3,)),
        ],
        compiler_params=PARAMS,
    )(packed, pin(lengths.reshape(1, per_dev)), pin(query), pin(cache))
    packed, got, early_q = lax.optimization_barrier((packed, got, early_q))
    mine = lax.cond(
        lower,
        lambda packed, got: fold(got[:, :, :span]),
        lambda packed, got: fold(exchange(packed)),
        packed, got,
    )
    mine, lengths, query, cache = lax.optimization_barrier((mine, lengths, query, cache))
    other = lax.ppermute(mine, "tp", swap)
    q_rows, stats = pl.pallas_call(
        late_kernel,
        out_shape=(heads_shape, stats_shape),
        in_specs=[VMEM] * 3,
        out_specs=(VMEM, VMEM),
        cost_estimate=pl.CostEstimate(flops=0, transcendentals=0, bytes_accessed=1 << 22),
        compiler_params=PARAMS,
    )(lengths.reshape(1, per_dev), query, cache)
    new_kv, attended = pl.pallas_call(
        functools.partial(merge_kernel, ranks),
        out_shape=(
            jax.ShapeDtypeStruct(kv_base.shape, BF16),
            jax.ShapeDtypeStruct(query.shape, BF16),
        ),
        in_specs=[VMEM] * 7,
        out_specs=(VMEM, VMEM),
        scratch_shapes=[pltpu.VMEM((per_dev * heads, HD), F32)],
        compiler_params=PARAMS,
    )(mine, other, q_rows, stats, early_q, early_stats, kv_base)
    return (new_kv, attended)


def solution(mesh):
    placed = (
        P(("group", "req"), None),
        P("group"),
        P(),
        P(("group", "req")),
        P(("group", "req"), "tp"),
        P(("group", "req"), None),
        P(("group", "req"), None, None),
        P("req", "tp"),
        P("req", "tp", None),
    )
    return jax.shard_map(
        shards,
        mesh=mesh,
        in_specs=placed,
        out_specs=(P(("group", "req"), None), P(("group", "req"), "tp")),
        check_vma=False,
    )
```

```python
import functools

import jax
import jax.numpy as jnp
from jax import lax
from jax.experimental import pallas as pl
from jax.experimental.pallas import tpu as pltpu
from jax.sharding import PartitionSpec as P

HD = 128
ADAPTERS = 64
F32 = jnp.float32
BF16 = jnp.bfloat16
VMEM = pl.BlockSpec(memory_space=pltpu.VMEM)
SMEM = pl.BlockSpec(memory_space=pltpu.SMEM)
HBM = pl.BlockSpec(memory_space=pltpu.HBM)
PARAMS = pltpu.CompilerParams(vmem_limit_bytes=8 * 1024 * 1024)


def iota(shape, dim):
    return lax.broadcasted_iota(jnp.int32, shape, dim)


def one_hot_ids(ids):
    shape = (ADAPTERS, ids.shape[1])
    return (iota(shape, 0) == jnp.broadcast_to(ids, shape)).astype(BF16)


def across(a, b):
    return lax.dot_general(a, b, (((0,), (0,)), ((), ())), preferred_element_type=F32)


def runs(order):
    found = []
    for p, q in enumerate(order):
        if p and q == order[p - 1] + 1:
            found[-1] = (found[-1][0], found[-1][1] + 1)
        else:
            found.append((p, 1))
    return found


def start_kernel(
    order, hidden_ref, ids_hbm, home_hbm, up_hbm, out_ref, ids_ref, home_ref, up_ref, sems
):
    parts, _, block = hidden_ref.shape

    @pl.when(lax.axis_index("tp") == 1)
    def _():
        copies = [
            *(
                pltpu.make_async_copy(
                    hidden_ref.at[pl.ds(order[at], count)],
                    out_ref.at[pl.ds(at, count), :, pl.ds(0, block)],
                    sems.at[5 + i],
                )
                for i, (at, count) in enumerate(runs(order))
            ),
            pltpu.make_async_copy(ids_hbm, ids_ref, sems.at[2]),
            pltpu.make_async_copy(home_hbm, home_ref, sems.at[3]),
            pltpu.make_async_copy(up_hbm, up_ref, sems.at[4]),
        ]
        for copy in copies:
            copy.start()
        for copy in copies:
            copy.wait()


def needed_rows(ids, home, up_ref, flat_ref, wide_ref):
    slots, ranks, width = up_ref.shape
    depth = flat_ref.shape[0]
    if depth > slots:
        flat_ref[...] = jnp.zeros_like(flat_ref)
    wide_ref[...] = up_ref[...].astype(F32)
    for r in range(ranks):
        flat_ref[:slots, r * width : (r + 1) * width] = wide_ref[:, r, :]
    shape = (depth, ADAPTERS)
    base = lax.axis_index("req").astype(jnp.int32) * slots
    here = jnp.broadcast_to(home, shape) - base == iota(shape, 0)
    held = here & (iota(shape, 0) < slots)
    match = jnp.dot(held.astype(BF16), one_hot_ids(ids), preferred_element_type=F32)
    return across(match.astype(BF16), flat_ref[...].astype(BF16)).astype(BF16)


def pack_kernel(
    order, blocks_ref, ids_hbm, home_hbm, up_hbm, cache_hbm, down_hbm, *rest
):
    pack(order, blocks_ref, ids_hbm, home_hbm, up_hbm, *rest[2:])


def pack(
    order, blocks_ref, ids_hbm, home_hbm, up_hbm, out_ref,
    ids_ref, home_ref, up_ref, flat_ref, wide_ref, sems
):
    count = out_ref.shape[1]
    span = flat_ref.shape[1]
    lower = lax.axis_index("tp") == 0

    @pl.when(lower)
    def _():
        pairs = ((ids_hbm, ids_ref), (home_hbm, home_ref), (up_hbm, up_ref))
        copies = [pltpu.make_async_copy(a, b, sems.at[i]) for i, (a, b) in enumerate(pairs)]
        for copy in copies:
            copy.start()
        for copy in copies:
            copy.wait()
        rows = needed_rows(ids_ref[...], home_ref[...], up_ref, flat_ref, wide_ref)
        for p, q in enumerate(order):
            out_ref[p, :, :span] = rows[q * count : (q + 1) * count]


def low_kernel(
    order, ids_ref, home_ref, up_ref, got_ref, down_ref, far_ref, out_ref, flat_ref, wide_ref
):
    parts, per_dev, _ = out_ref.shape
    block, columns = down_ref.shape
    ranks = columns // ADAPTERS
    span = flat_ref.shape[1]

    @pl.when(lax.axis_index("tp") == 1)
    def _():
        pieces = [got_ref[p].astype(F32)[:, :block] for p in range(parts)]
        blocks = jnp.concatenate(pieces, axis=0).astype(BF16)
        names = across(one_hot_ids(ids_ref[...]), iota((ADAPTERS, 128), 0).astype(BF16))
        names = names.astype(jnp.int32)
        names = jnp.concatenate(
            [
                names[order[at] * per_dev : (order[at] + count) * per_dev]
                for at, count in runs(order)
            ],
            axis=0,
        )
        lane = iota(names.shape, 1)
        spot = names + lane % 2 * ADAPTERS
        rank = lane % (2 * ranks)
        low = jnp.zeros(names.shape, F32)
        for half, ref in enumerate((far_ref, down_ref)):
            for j in range(columns // 128):
                values = jnp.dot(
                    blocks, ref[:, j * 128 : (j + 1) * 128], preferred_element_type=F32
                )
                got = jnp.take_along_axis(values, spot, axis=1)
                low = jnp.where(rank // 2 == j + half * ranks // 2, got, low)
        high = low.astype(BF16).astype(F32)
        low = jnp.where(lane < 2 * ranks, high, low - high).astype(BF16)
        rows = needed_rows(ids_ref[...], home_ref[...], up_ref, flat_ref, wide_ref)
        for p, q in enumerate(order):
            out_ref[p, :, :span] = rows[q * per_dev : (q + 1) * per_dev]
            out_ref[p, :, span:] = low[p * per_dev : (p + 1) * per_dev]


def fold_kernel(ranks, span, got_ref, out_ref, wide_ref):
    total = got_ref[0].astype(F32)
    for p in range(1, got_ref.shape[0]):
        total = total + got_ref[p].astype(F32)
    count = total.shape[0]
    tall = span // HD * count
    for j in range(span // HD):
        wide_ref[j * count : (j + 1) * count, :] = total[:, j * HD : (j + 1) * HD]
    out_ref[:tall, :] = wide_ref[...].astype(BF16)
    if total.shape[1] == span + 128:
        low = total[:, span:]
        low = low + pltpu.roll(low, 128 - 2 * ranks, 1)
        out_ref[tall:, :] = jnp.concatenate([low] * (16 // count), axis=0).astype(BF16)


def middle_kernel(
    order, ids_ref, home_ref, up_ref, got_ref, down_ref, far_ref, lengths_hbm, query_hbm,
    cache_hbm, out_ref, q_ref, stats_ref, flat_ref, wide_ref, lengths_ref, query_ref,
    cache_ref, sems
):
    low_kernel(
        order, ids_ref, home_ref, up_ref, got_ref, down_ref, far_ref, out_ref, flat_ref, wide_ref
    )

    @pl.when(lax.axis_index("tp") == 0)
    def _():
        early(lengths_hbm, query_hbm, cache_hbm, q_ref, stats_ref,
              lengths_ref, query_ref, cache_ref, sems)


def early(
    lengths_hbm, query_hbm, cache_hbm, q_ref, stats_ref, lengths_ref, query_ref, cache_ref, sems
):
    pairs = ((lengths_hbm, lengths_ref), (query_hbm, query_ref), (cache_hbm, cache_ref))
    copies = [pltpu.make_async_copy(a, b, sems.at[i]) for i, (a, b) in enumerate(pairs)]
    for copy in copies:
        copy.start()
    for copy in copies:
        copy.wait()
    attend(lengths_ref, query_ref, cache_ref, q_ref, stats_ref)


def late_kernel(lengths_ref, query_ref, cache_ref, q_ref, stats_ref):
    @pl.when(lax.axis_index("tp") == 1)
    def _():
        attend(lengths_ref, query_ref, cache_ref, q_ref, stats_ref)


def attend(lengths_ref, query_ref, cache_ref, q_ref, stats_ref):
    count = cache_ref.shape[0]
    heads = query_ref.shape[1] // HD
    scale = HD ** (-0.5)
    query = query_ref[...].astype(F32)
    lengths = lengths_ref[...]
    for h in range(heads):
        q_ref[pl.ds(h, count, stride=heads), :] = query[:, h * HD : (h + 1) * HD]
    for b in range(count):
        part = slice(b * heads, (b + 1) * heads)
        scores = lax.dot_general(
            q_ref[part, :].astype(BF16),
            cache_ref[b, :, :HD],
            (((1,), (1,)), ((), ())),
            preferred_element_type=F32,
        )
        valid = iota(scores.shape, 1) < lengths[:, b : b + 1]
        scores = jnp.where(valid, scores * scale, -jnp.inf)
        top = jnp.max(scores, axis=1, keepdims=True)
        weights = jnp.exp(scores - top)
        total = jnp.sum(weights, axis=1, keepdims=True)
        acc = jnp.dot(weights.astype(BF16), cache_ref[b, :, HD:], preferred_element_type=F32)
        stats_ref[part, :] = acc / total
        after = slice((count + b) * heads, (count + b + 1) * heads)
        stats_ref[after, :] = jnp.broadcast_to(top + jnp.log(total), acc.shape)


def merge_kernel(
    ranks, mine_ref, other_ref, q_ref, stats_ref, early_q_ref, early_ref, base_ref,
    kv_ref, out_ref, wide_ref
):
    count, width = base_ref.shape
    rows = q_ref.shape[0]
    heads = rows // count
    halves = width // HD
    tile = halves * count
    span = ranks * tile
    lower = lax.axis_index("tp") == 0
    base = base_ref[...].astype(F32)
    fresh = jnp.concatenate([base[:, j * HD : (j + 1) * HD] for j in range(halves)], axis=0)
    low = jnp.where(lower, other_ref[span:, :], mine_ref[span:, :]).astype(F32)[:tile]
    for r in range(0, ranks, 16 // tile):
        part = slice(r * tile, r * tile + 16)
        mine = mine_ref[part, :]
        other = other_ref[part, :]
        for half, pair in ((0, jnp.where(lower, mine, other)), (1, jnp.where(lower, other, mine))):
            pair = pair.astype(F32)
            for i in range(16 // tile):
                at = half * ranks + r + i
                fresh = fresh + low[:, at : at + 1] * pair[i * tile : (i + 1) * tile]
    fresh = fresh.astype(BF16).astype(F32)
    for j in range(halves):
        kv_ref[:, j * HD : (j + 1) * HD] = fresh[j * count : (j + 1) * count].astype(BF16)
    stats = jnp.where(lower, early_ref[...], stats_ref[...])
    query = jnp.where(lower, early_q_ref[...], q_ref[...])
    mean = stats[:rows]
    level = stats[rows:, :1]
    spread = [
        jnp.concatenate(
            [
                jnp.broadcast_to(fresh[j * count + b : j * count + b + 1], (heads, HD))
                for b in range(count)
            ],
            axis=0,
        )
        for j in range(halves)
    ]
    own = jnp.sum(query * spread[0], axis=1, keepdims=True) * HD ** (-0.5)
    share = 1.0 / (1.0 + jnp.exp(level - own))
    wide_ref[...] = mean + share * (spread[1] - mean)
    for h in range(heads):
        out_ref[:, h * HD : (h + 1) * HD] = wide_ref[pl.ds(h, count, stride=heads), :].astype(BF16)


def shards(
    hidden, adapter_ids, home_slot, lengths, query, kv_base, cache, adapter_down, adapter_up
):
    per_dev = hidden.shape[0]
    slots, ranks, width = adapter_up.shape
    parts = lax.axis_size("req")
    everyone = per_dev * parts
    block = hidden.shape[1] // parts
    heads = query.shape[1] // HD
    span = ranks * width
    wide = max(block, span)
    center = (parts // 2 + 1) % parts
    order = [center, 0, *range(center + 1, parts), *range(1, center)] if center else [*range(parts)]
    depth = -(-slots // 8) * 8
    core = lax.axis_index("tp").astype(jnp.int32)
    swap = [(0, 1), (1, 0)]
    blocks_shape = jax.ShapeDtypeStruct((parts, per_dev, wide), BF16)
    tall = span // HD * per_dev
    trade_shape = jax.ShapeDtypeStruct((tall + 16, HD), BF16)

    def pin(x):
        return pltpu.with_memory_space_constraint(x, pltpu.HBM)

    def exchange(x):
        return lax.all_to_all(
            x, "req", split_axis=0, concat_axis=0, tiled=True, axis_index_groups=[order]
        )

    ids = adapter_ids.reshape(1, everyone)
    home = home_slot.reshape(1, ADAPTERS)
    like = lambda x: jax.ShapeDtypeStruct(x.shape, x.dtype)
    blocks, near_ids, near_home, near_up = pl.pallas_call(
        functools.partial(start_kernel, order),
        out_shape=(blocks_shape, like(ids), like(home), like(adapter_up)),
        in_specs=[HBM] * 4,
        out_specs=(VMEM,) * 4,
        scratch_shapes=[pltpu.SemaphoreType.DMA((5 + len(runs(order)),))],
        compiler_params=PARAMS,
    )(
        pin(jnp.swapaxes(hidden.reshape(per_dev, parts, block), 0, 1)),
        pin(ids),
        pin(home),
        pin(adapter_up),
    )
    blocks, near_down, lower = lax.optimization_barrier((blocks, adapter_down, core == 0))
    far_down = lax.ppermute(near_down, "tp", swap)
    blocks = pl.pallas_call(
        functools.partial(pack_kernel, order),
        out_shape=blocks_shape,
        in_specs=[VMEM] + [HBM] * 7,
        out_specs=VMEM,
        scratch_shapes=[
            pltpu.VMEM(ids.shape, ids.dtype),
            pltpu.VMEM(home.shape, home.dtype),
            pltpu.VMEM(adapter_up.shape, BF16),
            pltpu.VMEM((depth, span), F32),
            pltpu.VMEM((slots, ranks, width), F32),
            pltpu.SemaphoreType.DMA((3,)),
        ],
        input_output_aliases={0: 0},
        compiler_params=PARAMS,
    )(
        blocks, pin(ids), pin(home), pin(adapter_up),
        pin(cache), pin(near_down), pin(cache), pin(near_down),
    )
    got = exchange(blocks)
    heads_shape = jax.ShapeDtypeStruct((per_dev * heads, HD), F32)
    stats_shape = jax.ShapeDtypeStruct((2 * per_dev * heads, HD), F32)
    packed, early_q, early_stats = pl.pallas_call(
        functools.partial(middle_kernel, order),
        out_shape=(
            jax.ShapeDtypeStruct((parts, per_dev, span + 128), BF16), heads_shape, stats_shape
        ),
        in_specs=[VMEM] * 6 + [HBM] * 3,
        out_specs=(VMEM,) * 3,
        scratch_shapes=[
            pltpu.VMEM((depth, span), F32),
            pltpu.VMEM((slots, ranks, width), F32),
            pltpu.VMEM((1, per_dev), lengths.dtype),
            pltpu.VMEM(query.shape, BF16),
            pltpu.VMEM(cache.shape, BF16),
            pltpu.SemaphoreType.DMA((3,)),
        ],
        compiler_params=PARAMS,
    )(
        near_ids, near_home, near_up, got, near_down, far_down,
        pin(lengths.reshape(1, per_dev)), pin(query), pin(cache),
    )
    packed, got, lower = lax.optimization_barrier((packed, got, lower))

    def fold(x):
        return pl.pallas_call(
            functools.partial(fold_kernel, ranks, span),
            out_shape=trade_shape,
            in_specs=[VMEM],
            out_specs=VMEM,
            scratch_shapes=[pltpu.VMEM((tall, HD), F32)],
            compiler_params=PARAMS,
        )(x)

    mine = lax.cond(
        lower,
        lambda packed, got: fold(got[:, :, :span]),
        lambda packed, got: fold(exchange(packed)),
        packed, got,
    )
    mine, lengths, query, cache = lax.optimization_barrier((mine, lengths, query, cache))
    other = lax.ppermute(mine, "tp", swap)
    q_rows, stats = pl.pallas_call(
        late_kernel,
        out_shape=(heads_shape, stats_shape),
        in_specs=[VMEM] * 3,
        out_specs=(VMEM, VMEM),
        cost_estimate=pl.CostEstimate(flops=0, transcendentals=0, bytes_accessed=1 << 22),
        compiler_params=PARAMS,
    )(lengths.reshape(1, per_dev), query, cache)
    new_kv, attended = pl.pallas_call(
        functools.partial(merge_kernel, ranks),
        out_shape=(
            jax.ShapeDtypeStruct(kv_base.shape, BF16),
            jax.ShapeDtypeStruct(query.shape, BF16),
        ),
        in_specs=[VMEM] * 7,
        out_specs=(VMEM, VMEM),
        scratch_shapes=[pltpu.VMEM((per_dev * heads, HD), F32)],
        compiler_params=PARAMS,
    )(mine, other, q_rows, stats, early_q, early_stats, kv_base)
    return (new_kv, attended)


def solution(mesh):
    placed = (
        P(("group", "req"), None),
        P("group"),
        P(),
        P(("group", "req")),
        P(("group", "req"), "tp"),
        P(("group", "req"), None),
        P(("group", "req"), None, None),
        P("req", "tp"),
        P("req", "tp", None),
    )
    return jax.shard_map(
        shards,
        mesh=mesh,
        in_specs=placed,
        out_specs=(P(("group", "req"), None), P(("group", "req"), "tp")),
        check_vma=False,
    )
```

```python
import functools

import jax
import jax.numpy as jnp
from jax import lax
from jax.experimental import pallas as pl
from jax.experimental.pallas import tpu as pltpu
from jax.sharding import PartitionSpec as P

HD = 128
ADAPTERS = 64
F32 = jnp.float32
BF16 = jnp.bfloat16
VMEM = pl.BlockSpec(memory_space=pltpu.VMEM)
SMEM = pl.BlockSpec(memory_space=pltpu.SMEM)
HBM = pl.BlockSpec(memory_space=pltpu.HBM)
PARAMS = pltpu.CompilerParams(vmem_limit_bytes=8 * 1024 * 1024)


def iota(shape, dim):
    return lax.broadcasted_iota(jnp.int32, shape, dim)


def one_hot_ids(ids):
    shape = (ADAPTERS, ids.shape[1])
    return (iota(shape, 0) == jnp.broadcast_to(ids, shape)).astype(BF16)


def across(a, b):
    return lax.dot_general(a, b, (((0,), (0,)), ((), ())), preferred_element_type=F32)


def runs(order):
    found = []
    for p, q in enumerate(order):
        if p and q == order[p - 1] + 1:
            found[-1] = (found[-1][0], found[-1][1] + 1)
        else:
            found.append((p, 1))
    return found


def start_kernel(
    order, hidden_ref, ids_hbm, home_hbm, up_hbm, out_ref, ids_ref, home_ref, up_ref, sems
):
    parts, _, block = hidden_ref.shape

    @pl.when(lax.axis_index("tp") == 1)
    def _():
        copies = [
            *(
                pltpu.make_async_copy(
                    hidden_ref.at[pl.ds(order[at], count)],
                    out_ref.at[pl.ds(at, count), :, pl.ds(0, block)],
                    sems.at[5 + i],
                )
                for i, (at, count) in enumerate(runs(order))
            ),
            pltpu.make_async_copy(ids_hbm, ids_ref, sems.at[2]),
            pltpu.make_async_copy(home_hbm, home_ref, sems.at[3]),
            pltpu.make_async_copy(up_hbm, up_ref, sems.at[4]),
        ]
        for copy in copies:
            copy.start()
        for copy in copies:
            copy.wait()


def needed_rows(ids, home, up_ref, flat_ref, wide_ref):
    slots, ranks, width = up_ref.shape
    depth = flat_ref.shape[0]
    if depth > slots:
        flat_ref[...] = jnp.zeros_like(flat_ref)
    wide_ref[...] = up_ref[...].astype(F32)
    for r in range(ranks):
        flat_ref[:slots, r * width : (r + 1) * width] = wide_ref[:, r, :]
    shape = (depth, ADAPTERS)
    base = lax.axis_index("req").astype(jnp.int32) * slots
    here = jnp.broadcast_to(home, shape) - base == iota(shape, 0)
    held = here & (iota(shape, 0) < slots)
    match = jnp.dot(held.astype(BF16), one_hot_ids(ids), preferred_element_type=F32)
    return across(match.astype(BF16), flat_ref[...].astype(BF16)).astype(BF16)


def pack_kernel(
    order, blocks_ref, ids_hbm, home_hbm, up_hbm, cache_hbm, down_hbm, *rest
):
    pack(order, blocks_ref, ids_hbm, home_hbm, up_hbm, *rest[2:])


def pack(
    order, blocks_ref, ids_hbm, home_hbm, up_hbm, out_ref,
    ids_ref, home_ref, up_ref, flat_ref, wide_ref, sems
):
    count = out_ref.shape[1]
    span = flat_ref.shape[1]
    lower = lax.axis_index("tp") == 0

    @pl.when(lower)
    def _():
        pairs = ((ids_hbm, ids_ref), (home_hbm, home_ref), (up_hbm, up_ref))
        copies = [pltpu.make_async_copy(a, b, sems.at[i]) for i, (a, b) in enumerate(pairs)]
        for copy in copies:
            copy.start()
        for copy in copies:
            copy.wait()
        rows = needed_rows(ids_ref[...], home_ref[...], up_ref, flat_ref, wide_ref)
        for p, q in enumerate(order):
            out_ref[p, :, :span] = rows[q * count : (q + 1) * count]


def low_kernel(
    order, ids_ref, home_ref, up_ref, got_ref, down_ref, far_ref, out_ref, flat_ref, wide_ref
):
    parts, per_dev, _ = out_ref.shape
    block, columns = down_ref.shape
    ranks = columns // ADAPTERS
    span = flat_ref.shape[1]

    @pl.when(lax.axis_index("tp") == 1)
    def _():
        rows = needed_rows(ids_ref[...], home_ref[...], up_ref, flat_ref, wide_ref)
        for p, q in enumerate(order):
            out_ref[p, :, :span] = rows[q * per_dev : (q + 1) * per_dev]
        pieces = [got_ref[p].astype(F32)[:, :block] for p in range(parts)]
        blocks = jnp.concatenate(pieces, axis=0).astype(BF16)
        names = across(one_hot_ids(ids_ref[...]), iota((ADAPTERS, 128), 0).astype(BF16))
        names = names.astype(jnp.int32)
        names = jnp.concatenate(
            [
                names[order[at] * per_dev : (order[at] + count) * per_dev]
                for at, count in runs(order)
            ],
            axis=0,
        )
        lane = iota(names.shape, 1)
        spot = names + lane % 2 * ADAPTERS
        rank = lane % (2 * ranks)
        low = jnp.zeros(names.shape, F32)
        for half, ref in enumerate((far_ref, down_ref)):
            for j in range(columns // 128):
                values = jnp.dot(
                    blocks, ref[:, j * 128 : (j + 1) * 128], preferred_element_type=F32
                )
                got = jnp.take_along_axis(values, spot, axis=1)
                low = jnp.where(rank // 2 == j + half * ranks // 2, got, low)
        high = low.astype(BF16).astype(F32)
        low = jnp.where(lane < 2 * ranks, high, low - high).astype(BF16)
        for p in range(parts):
            out_ref[p, :, span:] = low[p * per_dev : (p + 1) * per_dev]


def fold_kernel(ranks, span, got_ref, out_ref, wide_ref):
    total = got_ref[0].astype(F32)
    for p in range(1, got_ref.shape[0]):
        total = total + got_ref[p].astype(F32)
    count = total.shape[0]
    tall = span // HD * count
    for j in range(span // HD):
        wide_ref[j * count : (j + 1) * count, :] = total[:, j * HD : (j + 1) * HD]
    out_ref[:tall, :] = wide_ref[...].astype(BF16)
    if total.shape[1] == span + 128:
        low = total[:, span:]
        low = low + pltpu.roll(low, 128 - 2 * ranks, 1)
        out_ref[tall:, :] = jnp.concatenate([low] * (16 // count), axis=0).astype(BF16)


def early_kernel(
    low_ref, lengths_hbm, query_hbm, cache_hbm, q_ref, stats_ref,
    lengths_ref, query_ref, cache_ref, sems
):
    @pl.when(lax.axis_index("tp") == 0)
    def _():
        early(lengths_hbm, query_hbm, cache_hbm, q_ref, stats_ref,
              lengths_ref, query_ref, cache_ref, sems)


def early(
    lengths_hbm, query_hbm, cache_hbm, q_ref, stats_ref, lengths_ref, query_ref, cache_ref, sems
):
    pairs = ((lengths_hbm, lengths_ref), (query_hbm, query_ref), (cache_hbm, cache_ref))
    copies = [pltpu.make_async_copy(a, b, sems.at[i]) for i, (a, b) in enumerate(pairs)]
    for copy in copies:
        copy.start()
    for copy in copies:
        copy.wait()
    attend(lengths_ref, query_ref, cache_ref, q_ref, stats_ref)


def late_kernel(lengths_ref, query_ref, cache_ref, q_ref, stats_ref):
    @pl.when(lax.axis_index("tp") == 1)
    def _():
        attend(lengths_ref, query_ref, cache_ref, q_ref, stats_ref)


def attend(lengths_ref, query_ref, cache_ref, q_ref, stats_ref):
    count = cache_ref.shape[0]
    heads = query_ref.shape[1] // HD
    scale = HD ** (-0.5)
    query = query_ref[...].astype(F32)
    lengths = lengths_ref[...]
    for h in range(heads):
        q_ref[pl.ds(h, count, stride=heads), :] = query[:, h * HD : (h + 1) * HD]
    for b in range(count):
        part = slice(b * heads, (b + 1) * heads)
        scores = lax.dot_general(
            q_ref[part, :].astype(BF16),
            cache_ref[b, :, :HD],
            (((1,), (1,)), ((), ())),
            preferred_element_type=F32,
        )
        valid = iota(scores.shape, 1) < lengths[:, b : b + 1]
        scores = jnp.where(valid, scores * scale, -jnp.inf)
        top = jnp.max(scores, axis=1, keepdims=True)
        weights = jnp.exp(scores - top)
        total = jnp.sum(weights, axis=1, keepdims=True)
        acc = jnp.dot(weights.astype(BF16), cache_ref[b, :, HD:], preferred_element_type=F32)
        stats_ref[part, :] = acc / total
        after = slice((count + b) * heads, (count + b + 1) * heads)
        stats_ref[after, :] = jnp.broadcast_to(top + jnp.log(total), acc.shape)


def merge_kernel(
    ranks, mine_ref, other_ref, q_ref, stats_ref, early_q_ref, early_ref, base_ref,
    kv_ref, out_ref, wide_ref
):
    count, width = base_ref.shape
    rows = q_ref.shape[0]
    heads = rows // count
    halves = width // HD
    tile = halves * count
    span = ranks * tile
    lower = lax.axis_index("tp") == 0
    base = base_ref[...].astype(F32)
    fresh = jnp.concatenate([base[:, j * HD : (j + 1) * HD] for j in range(halves)], axis=0)
    low = jnp.where(lower, other_ref[span:, :], mine_ref[span:, :]).astype(F32)[:tile]
    for r in range(0, ranks, 16 // tile):
        part = slice(r * tile, r * tile + 16)
        mine = mine_ref[part, :]
        other = other_ref[part, :]
        for half, pair in ((0, jnp.where(lower, mine, other)), (1, jnp.where(lower, other, mine))):
            pair = pair.astype(F32)
            for i in range(16 // tile):
                at = half * ranks + r + i
                fresh = fresh + low[:, at : at + 1] * pair[i * tile : (i + 1) * tile]
    fresh = fresh.astype(BF16).astype(F32)
    for j in range(halves):
        kv_ref[:, j * HD : (j + 1) * HD] = fresh[j * count : (j + 1) * count].astype(BF16)
    stats = jnp.where(lower, early_ref[...], stats_ref[...])
    query = jnp.where(lower, early_q_ref[...], q_ref[...])
    mean = stats[:rows]
    level = stats[rows:, :1]
    spread = [
        jnp.concatenate(
            [
                jnp.broadcast_to(fresh[j * count + b : j * count + b + 1], (heads, HD))
                for b in range(count)
            ],
            axis=0,
        )
        for j in range(halves)
    ]
    own = jnp.sum(query * spread[0], axis=1, keepdims=True) * HD ** (-0.5)
    share = 1.0 / (1.0 + jnp.exp(level - own))
    wide_ref[...] = mean + share * (spread[1] - mean)
    for h in range(heads):
        out_ref[:, h * HD : (h + 1) * HD] = wide_ref[pl.ds(h, count, stride=heads), :].astype(BF16)


def shards(
    hidden, adapter_ids, home_slot, lengths, query, kv_base, cache, adapter_down, adapter_up
):
    per_dev = hidden.shape[0]
    slots, ranks, width = adapter_up.shape
    parts = lax.axis_size("req")
    everyone = per_dev * parts
    block = hidden.shape[1] // parts
    heads = query.shape[1] // HD
    span = ranks * width
    wide = max(block, span)
    center = (parts // 2 + 1) % parts
    order = [center, 0, *range(center + 1, parts), *range(1, center)] if center else [*range(parts)]
    depth = -(-slots // 8) * 8
    core = lax.axis_index("tp").astype(jnp.int32)
    swap = [(0, 1), (1, 0)]
    blocks_shape = jax.ShapeDtypeStruct((parts, per_dev, wide), BF16)
    tall = span // HD * per_dev
    trade_shape = jax.ShapeDtypeStruct((tall + 16, HD), BF16)

    def pin(x):
        return pltpu.with_memory_space_constraint(x, pltpu.HBM)

    def exchange(x):
        return lax.all_to_all(
            x, "req", split_axis=0, concat_axis=0, tiled=True, axis_index_groups=[order]
        )

    ids = adapter_ids.reshape(1, everyone)
    home = home_slot.reshape(1, ADAPTERS)
    like = lambda x: jax.ShapeDtypeStruct(x.shape, x.dtype)
    blocks, near_ids, near_home, near_up = pl.pallas_call(
        functools.partial(start_kernel, order),
        out_shape=(blocks_shape, like(ids), like(home), like(adapter_up)),
        in_specs=[HBM] * 4,
        out_specs=(VMEM,) * 4,
        scratch_shapes=[pltpu.SemaphoreType.DMA((5 + len(runs(order)),))],
        compiler_params=PARAMS,
    )(
        pin(jnp.swapaxes(hidden.reshape(per_dev, parts, block), 0, 1)),
        pin(ids),
        pin(home),
        pin(adapter_up),
    )
    blocks, near_down, lower = lax.optimization_barrier((blocks, adapter_down, core == 0))
    far_down = lax.ppermute(near_down, "tp", swap)
    blocks = pl.pallas_call(
        functools.partial(pack_kernel, order),
        out_shape=blocks_shape,
        in_specs=[VMEM] + [HBM] * 7,
        out_specs=VMEM,
        scratch_shapes=[
            pltpu.VMEM(ids.shape, ids.dtype),
            pltpu.VMEM(home.shape, home.dtype),
            pltpu.VMEM(adapter_up.shape, BF16),
            pltpu.VMEM((depth, span), F32),
            pltpu.VMEM((slots, ranks, width), F32),
            pltpu.SemaphoreType.DMA((3,)),
        ],
        input_output_aliases={0: 0},
        compiler_params=PARAMS,
    )(
        blocks, pin(ids), pin(home), pin(adapter_up),
        pin(cache), pin(near_down), pin(cache), pin(near_down),
    )
    got = exchange(blocks)
    packed = pl.pallas_call(
        functools.partial(low_kernel, order),
        out_shape=jax.ShapeDtypeStruct((parts, per_dev, span + 128), BF16),
        in_specs=[VMEM] * 6,
        out_specs=VMEM,
        scratch_shapes=[
            pltpu.VMEM((depth, span), F32),
            pltpu.VMEM((slots, ranks, width), F32),
        ],
        compiler_params=PARAMS,
    )(near_ids, near_home, near_up, got, near_down, far_down)

    packed, got, lower = lax.optimization_barrier((packed, got, lower))

    def fold(x):
        return pl.pallas_call(
            functools.partial(fold_kernel, ranks, span),
            out_shape=trade_shape,
            in_specs=[VMEM],
            out_specs=VMEM,
            scratch_shapes=[pltpu.VMEM((tall, HD), F32)],
            compiler_params=PARAMS,
        )(x)

    heads_shape = jax.ShapeDtypeStruct((per_dev * heads, HD), F32)
    stats_shape = jax.ShapeDtypeStruct((2 * per_dev * heads, HD), F32)

    early_q, early_stats = pl.pallas_call(
        early_kernel,
        out_shape=(heads_shape, stats_shape),
        in_specs=[VMEM] + [HBM] * 3,
        out_specs=(VMEM, VMEM),
        scratch_shapes=[
            pltpu.VMEM((1, per_dev), lengths.dtype),
            pltpu.VMEM(query.shape, BF16),
            pltpu.VMEM(cache.shape, BF16),
            pltpu.SemaphoreType.DMA((3,)),
        ],
        compiler_params=PARAMS,
    )(packed, pin(lengths.reshape(1, per_dev)), pin(query), pin(cache))
    packed, got, early_q = lax.optimization_barrier((packed, got, early_q))
    mine = lax.cond(
        lower,
        lambda packed, got: fold(got[:, :, :span]),
        lambda packed, got: fold(exchange(packed)),
        packed, got,
    )
    mine, lengths, query, cache = lax.optimization_barrier((mine, lengths, query, cache))
    other = lax.ppermute(mine, "tp", swap)
    q_rows, stats = pl.pallas_call(
        late_kernel,
        out_shape=(heads_shape, stats_shape),
        in_specs=[VMEM] * 3,
        out_specs=(VMEM, VMEM),
        cost_estimate=pl.CostEstimate(flops=0, transcendentals=0, bytes_accessed=1 << 22),
        compiler_params=PARAMS,
    )(lengths.reshape(1, per_dev), query, cache)
    new_kv, attended = pl.pallas_call(
        functools.partial(merge_kernel, ranks),
        out_shape=(
            jax.ShapeDtypeStruct(kv_base.shape, BF16),
            jax.ShapeDtypeStruct(query.shape, BF16),
        ),
        in_specs=[VMEM] * 7,
        out_specs=(VMEM, VMEM),
        scratch_shapes=[pltpu.VMEM((per_dev * heads, HD), F32)],
        compiler_params=PARAMS,
    )(mine, other, q_rows, stats, early_q, early_stats, kv_base)
    return (new_kv, attended)


def solution(mesh):
    placed = (
        P(("group", "req"), None),
        P("group"),
        P(),
        P(("group", "req")),
        P(("group", "req"), "tp"),
        P(("group", "req"), None),
        P(("group", "req"), None, None),
        P("req", "tp"),
        P("req", "tp", None),
    )
    return jax.shard_map(
        shards,
        mesh=mesh,
        in_specs=placed,
        out_specs=(P(("group", "req"), None), P(("group", "req"), "tp")),
        check_vma=False,
    )
```
